32 devices in a mesh: ctx: 16 (over z, x, core), head: 2 (over y).
Axes of the slice: x: 2, y: 2, z: 4, core: 2. Of those that a mesh axis runs over, the one named last changes fastest.
Arguments:
- queries: bfloat16 [6144, 64, 128], P(('ctx', 'head')), may hold values from -6 to 6
- keys: bfloat16 [6144, 64, 128], P(('ctx', 'head')), may hold values from -6 to 6
- values: bfloat16 [6144, 64, 128], P(('ctx', 'head')), may hold values from -6 to 6
- decay_log: bfloat16 [6144, 64], P(('ctx', 'head')), may hold values from -1 to 0, as said below
- out_gain: float32 [64, 128], replicated, may hold values from 0.1 to 1.9
Outputs:
- normed: bfloat16 [6144, 64, 128], P(('ctx', 'head'))
The draws below stay inside these ranges and needn't reach their ends.
Inputs may be any that keep to these rules, and one draw needn't show every extreme that they name: `decay_log`: every entry is negative or zero.
All inputs are finite; a program needn't handle non-finite values.
Results may differ from the reference program's by a relative error of at most 0.01.
Values may be sent and summed in bfloat16 or wider, within the bound.
A program may use at most 128 MiB of HBM per device.

```python
import jax
import jax.numpy as jnp
from jax import lax

HEAD_COUNT = 64
DH = 128
SEGMENT_TOKENS = 384
TOKEN_COUNT = 6144
N_CTX = 16


def correlated_pair(key):
    shared_key = jax.random.fold_in(key, 101)
    private_key = jax.random.fold_in(key, 202)
    full_shape = (TOKEN_COUNT, HEAD_COUNT, DH)
    shared = jax.random.normal(shared_key, full_shape, jnp.float32)
    private = jax.random.normal(private_key, full_shape, jnp.float32)
    keys_drawn = jnp.clip(shared, -6.0, 6.0)
    values_drawn = jnp.clip(0.8 * shared + 0.6 * private, -6.0, 6.0)
    return (keys_drawn, values_drawn)


def draw_keys(key, part):
    return correlated_pair(key)[0].astype(jnp.bfloat16)


def draw_values(key, part):
    return correlated_pair(key)[1].astype(jnp.bfloat16)


def draw_decay_log(key, part):
    complete_key_rows = jax.random.split(key, 7)
    order = jax.random.permutation(complete_key_rows[0], HEAD_COUNT)
    fast_count = HEAD_COUNT // 2
    rapid_decay = order < fast_count
    fast_rate = jnp.exp(jax.random.uniform(complete_key_rows[1], (HEAD_COUNT,), jnp.float32, jnp.log(1.0 / 50.0), jnp.log(1.0 / 30.0)))
    slow_rate = jnp.exp(jax.random.uniform(complete_key_rows[2], (HEAD_COUNT,), jnp.float32, jnp.log(0.05 / TOKEN_COUNT), jnp.log(0.5 / TOKEN_COUNT)))
    spike_rate = jnp.where(rapid_decay, fast_rate, slow_rate)
    random_offset = jax.random.uniform(complete_key_rows[3], (TOKEN_COUNT, HEAD_COUNT), jnp.float32, 0.5, 1.5)
    spike_position = jax.random.randint(complete_key_rows[4], (4, HEAD_COUNT), 0, TOKEN_COUNT)
    spike_retain = jax.random.uniform(complete_key_rows[5], (4, HEAD_COUNT), jnp.float32, 0.5, 0.8)
    token_position_index = jnp.arange(TOKEN_COUNT, dtype=jnp.int32)
    spike_flags = token_position_index[:, None, None] == spike_position[None, :, :]
    spike_logarithm = jnp.sum(jnp.where(spike_flags, jnp.log(spike_retain)[None], 0.0), axis=1)
    layer_output = jnp.maximum(-spike_rate[None, :] * random_offset + spike_logarithm, -1.0)
    spike_block_index = jax.random.randint(complete_key_rows[6], (), N_CTX - N_CTX // 4, N_CTX - 1)
    spike_first_token = spike_block_index * SEGMENT_TOKENS + SEGMENT_TOKENS - 6
    spike_token_offset = token_position_index - spike_first_token
    spike_marker_mask = (spike_token_offset >= 0) & (spike_token_offset < 6)
    strong_decay_mask = spike_marker_mask[:, None] & jnp.logical_not(rapid_decay)[None, :]
    layer_output = jnp.where(strong_decay_mask, -0.85, layer_output)
    return layer_output.astype(jnp.bfloat16)


def steps_of(stream_key, extent, shards, low, top_value):
    level = 1.0
    for axis_at, parts in shards:
        heights = jax.random.uniform(jax.random.fold_in(jax.random.fold_in(stream_key, 6), axis_at), (parts,), jnp.float32, low / len(shards), top_value / len(shards))
        level = level * jnp.repeat(jnp.exp(heights), extent[axis_at] // parts).reshape((-1,) + (1,) * (len(extent) - 1 - axis_at))
    return level


def gaussian(own_key, shape, scale, limit, cuts=(), held_as=jnp.bfloat16):
    gain = steps_of(own_key, shape, cuts, -0.22, 0.18) if cuts else 1.0
    values = jax.random.normal(own_key, shape, jnp.float32) * scale * gain
    return jnp.minimum(jnp.maximum(values, -limit), limit).astype(held_as)


def setup_inputs(seed: int = 0) -> dict:
    splits = jax.random.split(jax.random.key(seed), 6)
    queries = gaussian(splits[0], (TOKEN_COUNT, HEAD_COUNT, DH), 1.0, 6.0, ((0, 32),))
    keys = draw_keys(jax.random.fold_in(splits[5], 71), 0)
    values = draw_values(jax.random.fold_in(splits[5], 71), 0)
    decay_log = draw_decay_log(jax.random.fold_in(splits[5], 71), 0)
    out_gain = jnp.clip(1.0 + 0.18 * jax.random.normal(splits[4], (HEAD_COUNT, DH), jnp.float32), 0.1, 1.9)
    return {"queries": queries, "keys": keys, "values": values, "decay_log": decay_log, "out_gain": out_gain}


def activate(block):
    return jax.nn.silu(block.astype(jnp.float32)).astype(jnp.bfloat16)

def normalize(mixed, out_gain):
    values32 = mixed.astype(jnp.float32)
    meansq = lax.optimization_barrier(jnp.mean(values32 * values32, axis=(1, 2), keepdims=True))
    return (values32 * lax.rsqrt(meansq + 1e-06) * out_gain[None]).astype(jnp.bfloat16)

def make_step(out_gain):

    def span_step(state, pieces):
        queries_c, keys_c, values_c, decay_c = pieces
        query_act = activate(queries_c).astype(jnp.float32)
        key_act = activate(keys_c).astype(jnp.float32)
        value_act = activate(values_c).astype(jnp.float32)
        cumulative = jnp.cumsum(decay_c.astype(jnp.float32), axis=0)
        length = cumulative.shape[0]
        token_position_index = jnp.arange(length, dtype=jnp.int32)
        causal = (token_position_index[:, None] >= token_position_index[None, :])[None]
        scores = jnp.einsum('thd,shd->hts', query_act, key_act)
        offsets = cumulative.T[:, :, None] - cumulative.T[:, None, :]
        weights = jnp.where(causal, scores * jnp.exp(jnp.where(causal, offsets, -1e+30)), 0.0)
        weights = weights.astype(jnp.bfloat16).astype(jnp.float32)
        intra_out = jnp.einsum('hts,shd->thd', weights, value_act)
        ending = cumulative[-1]
        scaled_keys = (key_act * jnp.exp(ending[None, :] - cumulative)[:, :, None]).astype(jnp.bfloat16)
        local_state = jnp.einsum('shd,she->hde', scaled_keys.astype(jnp.float32), value_act)
        incoming_low = state.astype(jnp.bfloat16).astype(jnp.float32)
        inter_out = jnp.einsum('thd,hde->the', query_act, incoming_low) * jnp.exp(cumulative)[:, :, None]
        mixed = (intra_out + inter_out).astype(jnp.bfloat16)
        new_state = jnp.exp(ending)[:, None, None] * state + local_state
        return (new_state, normalize(mixed, out_gain))
    return span_step

def reference(queries, keys, values, decay_log, out_gain):
    blocked = (queries.reshape(N_CTX, SEGMENT_TOKENS, HEAD_COUNT, DH), keys.reshape(N_CTX, SEGMENT_TOKENS, HEAD_COUNT, DH), values.reshape(N_CTX, SEGMENT_TOKENS, HEAD_COUNT, DH), decay_log.reshape(N_CTX, SEGMENT_TOKENS, HEAD_COUNT))
    start = jnp.zeros((HEAD_COUNT, DH, DH), jnp.float32)
    final_state, normed = lax.scan(make_step(out_gain), start, blocked)
    return normed.reshape(TOKEN_COUNT, HEAD_COUNT, DH)
```

```python
import functools

import jax
import jax.numpy as jnp
from jax import lax
from jax.experimental import pallas as pl
from jax.experimental.pallas import tpu as pltpu
from jax.sharding import PartitionSpec as P

F32, BF16 = jnp.float32, jnp.bfloat16
MESH = pl.DeviceIdType.MESH
TILE = 128


def plan(n_ctx, n_head, heads):
    inner = 1
    for option in (2, 4):
        if n_ctx % option == 0 and heads % (option * n_head) == 0:
            inner = option
    group = inner * n_head
    per_owner = heads // group
    chunks = 1
    for option in (2, 4):
        if per_owner % option == 0 and (heads // option) % 16 == 0:
            chunks = option
    return inner, group, per_owner, chunks


def silu(x):
    half = 0.5 * x
    return half + half * jnp.tanh(half)


def kernel(
    n_ctx, n_head, q_hbm, k_hbm, v_hbm, dec_ref, mix_ref,
    q_in, k_in, v_in, tmp_a, tmp_b, q_hm, k_hm, v_hm, cum_b, cum_t, end_b, intra,
    ends, ends_in, s_out, s_in, pre, x_in, x_out, i_out, i_in, mix,
    in_sem, e_send, e_recv, s_send, s_recv, x_send, x_recv, i_send, i_recv, o_sem,
):
    rows, heads, dim = q_hbm.shape
    inner, group, per_owner, chunks = plan(n_ctx, n_head, heads)
    width = heads // chunks
    hc = per_owner // chunks
    planes = n_ctx // inner
    ctx, head = lax.axis_index("ctx"), lax.axis_index("head")
    plane = ctx // inner
    me = (ctx % inner) * n_head + head

    def device(peer):
        return (plane * inner + peer // n_head, peer % n_head)

    def peer_at(step):
        return lax.rem(me + step, group)

    def load(source, held, at, c):
        return pltpu.make_async_copy(
            source.at[:, pl.ds(c * width, width), :], held.at[c], in_sem.at[at, c]
        )

    for c in range(chunks):
        load(k_hbm, k_in, 0, c).start()
        load(v_hbm, v_in, 1, c).start()
    for c in range(chunks):
        load(q_hbm, q_in, 2, c).start()

    barrier = pltpu.get_barrier_semaphore()

    def greet(step, carry):
        pl.semaphore_signal(barrier, inc=1, device_id=device(peer_at(step)), device_id_type=MESH)
        return carry

    lax.fori_loop(1, group, greet, 0)
    if planes > 1:
        @pl.when(plane > 0)
        def _():
            pl.semaphore_signal(barrier, inc=1, device_id=(ctx - inner, head), device_id_type=MESH)

        @pl.when(plane < planes - 1)
        def _():
            pl.semaphore_signal(barrier, inc=1, device_id=(ctx + inner, head), device_id_type=MESH)

    decays = dec_ref[...]
    t_at = lax.broadcasted_iota(jnp.int32, (rows, rows), 0)
    s_at = lax.broadcasted_iota(jnp.int32, (rows, rows), 1)
    lower = jnp.where(s_at <= t_at, 1.0, 0.0).astype(BF16)
    upper = jnp.where(t_at <= s_at, 1.0, 0.0).astype(BF16)
    over_rows = (((0,), (0,)), ((), ()))
    cum_t[...] = lax.dot_general(decays, upper, over_rows, preferred_element_type=F32)
    end_b[...] = lax.dot_general(
        decays, jnp.ones((rows, dim), BF16), over_rows, preferred_element_type=F32
    )
    for o in range(group):
        for c in range(chunks):
            at = c * width + o * hc
            ends[o, c * hc : (c + 1) * hc, :] = end_b[at : at + hc, :]
    some = 8
    h_at = lax.broadcasted_iota(jnp.int32, (heads, some * dim), 0)
    l_at = lax.broadcasted_iota(jnp.int32, (heads, some * dim), 1) // dim

    def spread(g, carry):
        pick = jnp.where(h_at == l_at + g * some, 1.0, 0.0).astype(BF16)
        wide = jnp.dot(decays, pick, preferred_element_type=F32).astype(BF16)
        summed = jnp.dot(lower, wide, preferred_element_type=F32)
        for i in range(some):
            cum_b[g * some + i] = summed[:, i * dim : (i + 1) * dim]
        return carry

    lax.fori_loop(0, heads // some, spread, 0)

    greetings = group - 1
    if planes > 1:
        greetings = greetings + jnp.where(plane > 0, 1, 0) + jnp.where(plane < planes - 1, 1, 0)
    pl.semaphore_wait(barrier, greetings)

    def remote(src, dst, send, recv, to):
        return pltpu.make_async_remote_copy(
            src_ref=src, dst_ref=dst, send_sem=send, recv_sem=recv,
            device_id=to, device_id_type=MESH,
        )

    def end_copy(peer, slot):
        return remote(ends.at[peer], ends_in.at[slot], e_send.at[peer], e_recv.at[slot], device(peer))

    def s_copy(c, peer, slot):
        return remote(
            s_out.at[c, peer], s_in.at[c, slot], s_send.at[c, peer], s_recv.at[c, slot], device(peer)
        )

    def i_copy(c, peer, slot):
        return remote(
            i_out.at[c, peer], i_in.at[c, slot], i_send.at[c, peer], i_recv.at[c, slot], device(peer)
        )

    def x_copy(c):
        return remote(
            x_out.at[c], x_in.at[c], x_send.at[c], x_recv.at[c],
            (lax.rem(ctx + inner, n_ctx), head),
        )

    def each_peer(body):
        def one(step, carry):
            body(peer_at(step))
            return carry

        lax.fori_loop(1, group, one, 0)

    each_peer(lambda peer: end_copy(peer, me).start())
    ends_in[me] = ends[me]

    step_rows = 16

    def activate(held, c, tmp):
        def some_rows(b, carry):
            x = held[c, pl.ds(b * step_rows, step_rows)].astype(F32)
            tmp[pl.ds(b * step_rows * width, step_rows * width), :] = silu(x).reshape(
                step_rows * width, dim
            )
            return carry

        lax.fori_loop(0, rows // step_rows, some_rows, 0)

    unroll = 4

    def each_head(c, body):
        def one(g, carry):
            for u in range(unroll):
                i = g * unroll + u
                body(i, c * width + i)
            return carry

        lax.fori_loop(0, width // unroll, one, 0)

    def states(c):
        load(k_hbm, k_in, 0, c).wait()
        load(v_hbm, v_in, 1, c).wait()
        activate(k_in, c, tmp_a)
        activate(v_in, c, tmp_b)

        def one(i, h):
            key = tmp_a[pl.ds(i, rows, stride=width), :].astype(BF16)
            value = tmp_b[pl.ds(i, rows, stride=width), :].astype(BF16)
            k_hm[h] = key
            v_hm[h] = value
            fade = jnp.exp(end_b[pl.ds(h, 1), :] - cum_b[h])
            scaled = (key.astype(F32) * fade).astype(BF16)
            state = lax.dot_general(scaled, value, over_rows, preferred_element_type=F32)
            s_out[c, i // hc, pl.ds((i % hc) * dim, dim), :] = state.astype(BF16)

        each_head(c, one)
        each_peer(lambda peer: s_copy(c, peer, me).start())
        s_in[c, me] = s_out[c, me]

    def inside(c):
        load(q_hbm, q_in, 2, c).wait()
        activate(q_in, c, tmp_a)

        def one(i, h):
            query = tmp_a[pl.ds(i, rows, stride=width), :].astype(BF16)
            q_hm[h] = query
            key, value, cum = k_hm[h], v_hm[h], cum_b[h]
            row = cum_t[pl.ds(h, 1), :]
            outs = []
            for s0 in range(0, rows, TILE):
                w = min(TILE, rows - s0)
                n = rows - s0
                scores = lax.dot_general(
                    query[s0:], key[s0 : s0 + w], (((1,), (1,)), ((), ())),
                    preferred_element_type=F32,
                )
                offset = cum[s0:, :w] - row[:, s0 : s0 + w]
                tt = lax.broadcasted_iota(jnp.int32, (n, w), 0)
                ss = lax.broadcasted_iota(jnp.int32, (n, w), 1)
                weights = scores * jnp.exp(jnp.where(ss <= tt, offset, -1e30))
                outs.append(
                    jnp.dot(
                        weights.astype(BF16), value[s0 : s0 + w], preferred_element_type=F32
                    )
                )
            intra[h] = outs[0]
            for at in range(1, len(outs)):
                intra[h, at * TILE :, :] += outs[at]

        each_head(c, one)

    def join(c):
        each_peer(lambda peer: s_copy(c, peer, peer).wait_recv())

        def decay_of(j, i):
            return jnp.exp(ends_in[j, c * hc + i : c * hc + i + 1, :])

        for i in range(hc):
            part = pl.ds(i * dim, dim)
            total = s_in[c, 0, part, :].astype(F32)
            for j in range(1, group):
                pre[j, part, :] = total
                total = decay_of(j, i) * total + s_in[c, j, part, :].astype(F32)
            x_out[c, part, :] = total

        if planes > 1:
            @pl.when(plane > 0)
            def _():
                x_copy(c).wait_recv()
                for i in range(hc):
                    part = pl.ds(i * dim, dim)
                    fade = jnp.sum(ends_in[:, c * hc + i, :], axis=0, keepdims=True)
                    x_out[c, part, :] += jnp.exp(fade) * x_in[c, part, :]

            @pl.when(plane == 0)
            def _():
                x_in[c] = jnp.zeros(x_in.shape[1:], F32)

            @pl.when(plane < planes - 1)
            def _():
                x_copy(c).start()
        else:
            x_in[c] = jnp.zeros(x_in.shape[1:], F32)

        for i in range(hc):
            part = pl.ds(i * dim, dim)
            come = x_in[c, part, :]
            i_out[c, 0, part, :] = come.astype(BF16)
            fade = jnp.zeros((1, dim), F32)
            for j in range(1, group):
                fade = fade + ends_in[j - 1, c * hc + i : c * hc + i + 1, :]
                i_out[c, j, part, :] = (pre[j, part, :] + jnp.exp(fade) * come).astype(BF16)
        each_peer(lambda peer: i_copy(c, peer, me).start())
        i_in[c, me] = i_out[c, me]

    def finish(c):
        each_peer(lambda peer: i_copy(c, peer, peer).wait_recv())

        def one(i, h):
            come = i_in[c, i // hc, pl.ds((i % hc) * dim, dim), :]
            inter = jnp.dot(q_hm[h], come, preferred_element_type=F32)
            mix[pl.ds(h, rows, stride=heads), :] = intra[h] + inter * jnp.exp(cum_b[h])

        each_head(c, one)

    for c in range(chunks):
        states(c)
    each_peer(lambda peer: end_copy(peer, peer).wait_recv())
    for c in range(chunks):
        inside(c)
        join(c)
    for c in range(chunks):
        finish(c)

    def give(b, carry):
        span = step_rows * heads
        mix_ref[pl.ds(b * step_rows, step_rows)] = (
            mix[pl.ds(b * span, span), :].reshape(step_rows, heads, dim).astype(BF16)
        )
        return carry

    lax.fori_loop(0, rows // step_rows, give, 0)

    each_peer(lambda peer: end_copy(peer, me).wait_send())
    for c in range(chunks):
        each_peer(lambda peer: s_copy(c, peer, me).wait_send())
        each_peer(lambda peer: i_copy(c, peer, me).wait_send())
    if planes > 1:
        @pl.when(plane < planes - 1)
        def _():
            for c in range(chunks):
                x_copy(c).wait_send()


def normalize(mixed, out_gain):
    values32 = mixed.astype(F32)
    meansq = jnp.mean(values32 * values32, axis=(1, 2), keepdims=True)
    return (values32 * lax.rsqrt(meansq + 1e-06) * out_gain[None]).astype(BF16)


def shards(n_ctx, n_head, queries, keys, values, decay_log, out_gain):
    rows, heads, dim = queries.shape
    inner, group, per_owner, chunks = plan(n_ctx, n_head, heads)
    width, hc = heads // chunks, per_owner // chunks
    held = pltpu.VMEM((chunks, rows, width, dim), BF16)
    major = pltpu.VMEM((heads, rows, dim), BF16)
    block = (hc * dim, dim)
    dma = pltpu.SemaphoreType.DMA
    mixed = pl.pallas_call(
        functools.partial(kernel, n_ctx, n_head),
        out_shape=jax.ShapeDtypeStruct((rows, heads, dim), BF16),
        in_specs=[pl.BlockSpec(memory_space=pl.ANY)] * 3 + [pl.BlockSpec(memory_space=pltpu.VMEM)],
        out_specs=pl.BlockSpec(memory_space=pltpu.VMEM),
        scratch_shapes=[
            held, held, held,
            pltpu.VMEM((rows * width, dim), F32), pltpu.VMEM((rows * width, dim), F32),
            major, major, major,
            pltpu.VMEM((heads, rows, dim), F32),
            pltpu.VMEM((heads, rows), F32),
            pltpu.VMEM((heads, dim), F32),
            pltpu.VMEM((heads, rows, dim), F32),
            pltpu.VMEM((group, max(8, per_owner), dim), F32),
            pltpu.VMEM((group, max(8, per_owner), dim), F32),
            pltpu.VMEM((chunks, group) + block, BF16), pltpu.VMEM((chunks, group) + block, BF16),
            pltpu.VMEM((group,) + block, F32),
            pltpu.VMEM((chunks,) + block, F32), pltpu.VMEM((chunks,) + block, F32),
            pltpu.VMEM((chunks, group) + block, BF16), pltpu.VMEM((chunks, group) + block, BF16),
            pltpu.VMEM((rows * heads, dim), F32),
            dma((3, chunks)),
            dma((group,)), dma((group,)),
            dma((chunks, group)), dma((chunks, group)),
            dma((chunks,)), dma((chunks,)),
            dma((chunks, group)), dma((chunks, group)),
            dma,
        ],
        compiler_params=pltpu.CompilerParams(
            collective_id=0, has_side_effects=True, vmem_limit_bytes=60 * 2**20
        ),
        cost_estimate=pl.CostEstimate(
            flops=8 * rows * heads * dim * dim,
            bytes_accessed=8 * rows * heads * dim,
            transcendentals=0,
        ),
    )(queries, keys, values, decay_log)
    return normalize(mixed, out_gain)


def solution(mesh):
    return jax.shard_map(
        functools.partial(shards, mesh.shape["ctx"], mesh.shape["head"]),
        mesh=mesh,
        in_specs=(
            P(("ctx", "head"), None, None),
            P(("ctx", "head"), None, None),
            P(("ctx", "head"), None, None),
            P(("ctx", "head"), None),
            P(),
        ),
        out_specs=P(("ctx", "head"), None, None),
        check_vma=False,
    )
```

```python
import functools

import jax
import jax.numpy as jnp
from jax import lax
from jax.experimental import pallas as pl
from jax.experimental.pallas import tpu as pltpu
from jax.sharding import PartitionSpec as P

F32, BF16 = jnp.float32, jnp.bfloat16
MESH = pl.DeviceIdType.MESH
TILE = 128


def plan(n_ctx, n_head, heads):
    inner = 1
    for option in (2, 4):
        if n_ctx % option == 0 and heads % (option * n_head) == 0:
            inner = option
    group = inner * n_head
    per_owner = heads // group
    chunks = 1
    for option in (2, 4):
        if per_owner % option == 0 and (heads // option) % 16 == 0:
            chunks = option
    return inner, group, per_owner, chunks


def silu(x):
    half = 0.5 * x
    return half + half * jnp.tanh(half)


def kernel(
    n_ctx, n_head, q_hbm, k_hbm, v_hbm, dec_ref, mix_hbm, scale_ref,
    q_in, k_in, v_in, tmp_a, tmp_b, q_hm, k_hm, v_hm, cum_b, cum_t, end_b, intra,
    ends, ends_in, s_out, s_in, pre, tot_out, tot_in, t_out, t_in, come_x, i_out, i_in, squares,
    in_sem, e_send, e_recv, s_send, s_recv, d_send, d_recv, t_send, t_recv, i_send, i_recv, o_sem,
):
    rows, heads, dim = q_hbm.shape
    inner, group, per_owner, chunks = plan(n_ctx, n_head, heads)
    width = heads // chunks
    hc = per_owner // chunks
    planes = n_ctx // inner
    ctx, head = lax.axis_index("ctx"), lax.axis_index("head")
    plane = ctx // inner
    place = ctx % inner
    me = place * n_head + head

    def device(peer):
        return (plane * inner + peer // n_head, peer % n_head)

    def peer_at(step):
        return lax.rem(me + step, group)

    def load(source, held, at, c):
        return pltpu.make_async_copy(
            source.at[:, pl.ds(c * width, width), :], held.at[c], in_sem.at[at, c]
        )

    for c in range(chunks):
        load(k_hbm, k_in, 0, c).start()
        load(v_hbm, v_in, 1, c).start()
    for c in range(chunks):
        load(q_hbm, q_in, 2, c).start()

    barrier = pltpu.get_barrier_semaphore()

    def greet(step, carry):
        pl.semaphore_signal(barrier, inc=1, device_id=device(peer_at(step)), device_id_type=MESH)
        return carry

    lax.fori_loop(1, group, greet, 0)

    def greet_plane(step, carry):
        other = lax.rem(plane + step, planes)
        pl.semaphore_signal(
            barrier, inc=1, device_id=(other * inner + place, head), device_id_type=MESH
        )
        return carry

    lax.fori_loop(1, planes, greet_plane, 0)

    decays = dec_ref[...]
    t_at = lax.broadcasted_iota(jnp.int32, (rows, rows), 0)
    s_at = lax.broadcasted_iota(jnp.int32, (rows, rows), 1)
    lower = jnp.where(s_at <= t_at, 1.0, 0.0).astype(BF16)
    upper = jnp.where(t_at <= s_at, 1.0, 0.0).astype(BF16)
    over_rows = (((0,), (0,)), ((), ()))
    cum_t[...] = jnp.dot(decays, upper, preferred_element_type=F32)
    end_b[...] = jnp.dot(decays, jnp.ones((rows, dim), BF16), preferred_element_type=F32)
    for o in range(group):
        for c in range(chunks):
            at = c * width + o * hc
            ends[o, c * hc : (c + 1) * hc, :] = end_b[at : at + hc, :]
    squares[...] = jnp.zeros_like(squares)
    some = 8
    h_at = lax.broadcasted_iota(jnp.int32, (heads, some * dim), 0)
    l_at = lax.broadcasted_iota(jnp.int32, (heads, some * dim), 1) // dim

    def spread(g, carry):
        pick = jnp.where(h_at == l_at + g * some, 1.0, 0.0).astype(BF16)
        wide = lax.dot_general(
            decays, pick, over_rows, preferred_element_type=F32
        ).astype(BF16)
        summed = jnp.dot(lower, wide, preferred_element_type=F32)
        for i in range(some):
            cum_b[g * some + i] = summed[:, i * dim : (i + 1) * dim]
        return carry

    def remote(src, dst, send, recv, to):
        return pltpu.make_async_remote_copy(
            src_ref=src, dst_ref=dst, send_sem=send, recv_sem=recv,
            device_id=to, device_id_type=MESH,
        )

    def end_copy(peer, slot):
        return remote(ends.at[peer], ends_in.at[slot], e_send.at[peer], e_recv.at[slot], device(peer))

    def s_copy(c, peer, slot):
        return remote(
            s_out.at[c, peer], s_in.at[c, slot], s_send.at[c, peer], s_recv.at[c, slot], device(peer)
        )

    def i_copy(c, peer, slot):
        return remote(
            i_out.at[c, peer], i_in.at[c, slot], i_send.at[c, peer], i_recv.at[c, slot], device(peer)
        )

    def at_plane(other):
        return (other * inner + place, head)

    def d_copy(step, slot):
        other = lax.rem(plane + step, planes)
        return remote(tot_out, tot_in.at[slot], d_send.at[step], d_recv.at[slot], at_plane(other))

    def t_copy(c, step, slot):
        other = lax.rem(plane + step, planes)
        return remote(
            t_out.at[c], t_in.at[c, slot], t_send.at[c, step], t_recv.at[c, slot], at_plane(other)
        )

    def each_peer(body):
        def one(step, carry):
            body(peer_at(step))
            return carry

        lax.fori_loop(1, group, one, 0)

    def later_planes(body):
        for step in range(1, planes):
            @pl.when(plane + step < planes)
            def _():
                body(step)

    def earlier_planes(body):
        for p in range(planes - 1):
            @pl.when(p < plane)
            def _():
                body(p)

    step_rows = 16

    def activate(held, c, tmp):
        def some_rows(b, carry):
            x = held[c, pl.ds(b * step_rows, step_rows)].astype(F32)
            tmp[pl.ds(b * step_rows * width, step_rows * width), :] = silu(x).reshape(
                step_rows * width, dim
            )
            return carry

        lax.fori_loop(0, rows // step_rows, some_rows, 0)

    unroll = 4

    def each_head(c, body):
        def one(g, carry):
            for u in range(unroll):
                i = g * unroll + u
                body(i, c * width + i)
            return carry

        lax.fori_loop(0, width // unroll, one, 0)

    def states(c):
        lax.fori_loop(c * width // some, (c + 1) * width // some, spread, 0)
        load(k_hbm, k_in, 0, c).wait()
        load(v_hbm, v_in, 1, c).wait()
        activate(k_in, c, tmp_a)
        activate(v_in, c, tmp_b)

        def one(i, h):
            key = tmp_a[pl.ds(i, rows, stride=width), :].astype(BF16)
            value = tmp_b[pl.ds(i, rows, stride=width), :].astype(BF16)
            k_hm[h] = key
            v_hm[h] = value
            fade = jnp.exp(end_b[pl.ds(h, 1), :] - cum_b[h])
            scaled = (key.astype(F32) * fade).astype(BF16)
            state = lax.dot_general(scaled, value, over_rows, preferred_element_type=F32)
            s_out[c, i // hc, pl.ds((i % hc) * dim, dim), :] = state.astype(BF16)

        each_head(c, one)
        if c == 0:
            pl.semaphore_wait(barrier, group + planes - 2)
            each_peer(lambda peer: end_copy(peer, me).start())
            ends_in[me] = ends[me]
        each_peer(lambda peer: s_copy(c, peer, me).start())
        s_in[c, me] = s_out[c, me]

    def inside(c):
        load(q_hbm, q_in, 2, c).wait()
        activate(q_in, c, tmp_a)

        def one(i, h):
            query = tmp_a[pl.ds(i, rows, stride=width), :].astype(BF16)
            q_hm[h] = query
            key, value, cum = k_hm[h], v_hm[h], cum_b[h]
            row = cum_t[pl.ds(h, 1), :]
            outs = []
            for s0 in range(0, rows, TILE):
                w = min(TILE, rows - s0)
                n = rows - s0
                scores = lax.dot_general(
                    query[s0:], key[s0 : s0 + w], (((1,), (1,)), ((), ())),
                    preferred_element_type=F32,
                )
                offset = cum[s0:, :w] - row[:, s0 : s0 + w]
                tt = lax.broadcasted_iota(jnp.int32, (n, w), 0)
                ss = lax.broadcasted_iota(jnp.int32, (n, w), 1)
                weights = scores * jnp.exp(jnp.where(ss <= tt, offset, -1e30))
                outs.append(
                    jnp.dot(
                        weights.astype(BF16), value[s0 : s0 + w], preferred_element_type=F32
                    )
                )
            intra[h] = outs[0]
            for at in range(1, len(outs)):
                intra[h, at * TILE :, :] += outs[at]

        each_head(c, one)

    def join(c):
        if c == 0:
            each_peer(lambda peer: end_copy(peer, peer).wait_recv())
            tot_out[...] = jnp.sum(ends_in[...], axis=0)
            later_planes(lambda step: d_copy(step, plane).start())
        each_peer(lambda peer: s_copy(c, peer, peer).wait_recv())
        for i in range(hc):
            part = pl.ds(i * dim, dim)
            at = c * hc + i
            total = s_in[c, 0, part, :].astype(F32)
            for j in range(1, group):
                pre[c, j, part, :] = total
                fade = jnp.exp(ends_in[j, at : at + 1, :])
                total = fade * total + s_in[c, j, part, :].astype(F32)
            t_out[c, part, :] = total.astype(BF16)
        later_planes(lambda step: t_copy(c, step, plane).start())

    def spread_out(c):
        if c == 0:
            earlier_planes(lambda p: d_copy(1, p).wait_recv())
        earlier_planes(lambda p: t_copy(c, 1, p).wait_recv())
        come_x[...] = jnp.zeros_like(come_x)

        def add(p):
            for i in range(hc):
                part = pl.ds(i * dim, dim)
                at = c * hc + i
                fade = jnp.exp(tot_in[p, at : at + 1, :])
                come_x[part, :] = fade * come_x[part, :] + t_in[c, p, part, :].astype(F32)

        earlier_planes(add)
        for i in range(hc):
            part = pl.ds(i * dim, dim)
            at = c * hc + i
            come = come_x[part, :]
            i_out[c, 0, part, :] = come.astype(BF16)
            fade = jnp.zeros((1, dim), F32)
            for j in range(1, group):
                fade = fade + ends_in[j - 1, at : at + 1, :]
                i_out[c, j, part, :] = (pre[c, j, part, :] + jnp.exp(fade) * come).astype(BF16)
        each_peer(lambda peer: i_copy(c, peer, me).start())
        i_in[c, me] = i_out[c, me]

    def give(c):
        return pltpu.make_async_copy(
            q_in.at[c], mix_hbm.at[:, pl.ds(c * width, width), :], o_sem.at[c]
        )

    def finish(c):
        each_peer(lambda peer: i_copy(c, peer, peer).wait_recv())

        def one(i, h):
            come = i_in[c, i // hc, pl.ds((i % hc) * dim, dim), :]
            inter = jnp.dot(q_hm[h], come, preferred_element_type=F32)
            mixed = (intra[h] + inter * jnp.exp(cum_b[h])).astype(BF16).astype(F32)
            squares[...] += mixed * mixed
            tmp_a[pl.ds(i, rows, stride=width), :] = mixed

        each_head(c, one)

        def some_rows(b, carry):
            span = step_rows * width
            q_in[c, pl.ds(b * step_rows, step_rows)] = (
                tmp_a[pl.ds(b * span, span), :].reshape(step_rows, width, dim).astype(BF16)
            )
            return carry

        lax.fori_loop(0, rows // step_rows, some_rows, 0)
        give(c).start()

    for c in range(chunks):
        states(c)
    for c in range(chunks):
        join(c)
        inside(c)
        if c > 0:
            spread_out(c - 1)
    spread_out(chunks - 1)
    for c in range(chunks):
        finish(c)
    meansq = jnp.sum(squares[...], axis=1, keepdims=True) * (1.0 / (heads * dim))
    scale_ref[...] = jnp.broadcast_to(lax.rsqrt(meansq + 1e-06), scale_ref.shape)

    each_peer(lambda peer: end_copy(peer, me).wait_send())
    later_planes(lambda step: d_copy(step, plane).wait_send())
    for c in range(chunks):
        each_peer(lambda peer: s_copy(c, peer, me).wait_send())
        each_peer(lambda peer: i_copy(c, peer, me).wait_send())
        later_planes(lambda step: t_copy(c, step, plane).wait_send())
        give(c).wait()


def normalize(mixed, scale, out_gain):
    return (mixed.astype(F32) * scale[:, None, :] * out_gain[None]).astype(BF16)


def shards(n_ctx, n_head, queries, keys, values, decay_log, out_gain):
    rows, heads, dim = queries.shape
    inner, group, per_owner, chunks = plan(n_ctx, n_head, heads)
    width, hc = heads // chunks, per_owner // chunks
    held = pltpu.VMEM((chunks, rows, width, dim), BF16)
    major = pltpu.VMEM((heads, rows, dim), BF16)
    block = (hc * dim, dim)
    dma = pltpu.SemaphoreType.DMA
    planes = n_ctx // inner
    tile = (max(8, per_owner), dim)
    mixed, scale = pl.pallas_call(
        functools.partial(kernel, n_ctx, n_head),
        out_shape=(
            jax.ShapeDtypeStruct((rows, heads, dim), BF16),
            jax.ShapeDtypeStruct((rows, dim), F32),
        ),
        in_specs=[pl.BlockSpec(memory_space=pl.ANY)] * 3 + [pl.BlockSpec(memory_space=pltpu.VMEM)],
        out_specs=(pl.BlockSpec(memory_space=pl.ANY), pl.BlockSpec(memory_space=pltpu.VMEM)),
        scratch_shapes=[
            held, held, held,
            pltpu.VMEM((rows * width, dim), F32), pltpu.VMEM((rows * width, dim), F32),
            major, major, major,
            pltpu.VMEM((heads, rows, dim), F32),
            pltpu.VMEM((heads, rows), F32),
            pltpu.VMEM((heads, dim), F32),
            pltpu.VMEM((heads, rows, dim), F32),
            pltpu.VMEM((group,) + tile, F32), pltpu.VMEM((group,) + tile, F32),
            pltpu.VMEM((chunks, group) + block, BF16), pltpu.VMEM((chunks, group) + block, BF16),
            pltpu.VMEM((chunks, group) + block, F32),
            pltpu.VMEM(tile, F32), pltpu.VMEM((planes,) + tile, F32),
            pltpu.VMEM((chunks,) + block, BF16), pltpu.VMEM((chunks, planes) + block, BF16),
            pltpu.VMEM(block, F32),
            pltpu.VMEM((chunks, group) + block, BF16), pltpu.VMEM((chunks, group) + block, BF16),
            pltpu.VMEM((rows, dim), F32),
            dma((3, chunks)),
            dma((group,)), dma((group,)),
            dma((chunks, group)), dma((chunks, group)),
            dma((planes,)), dma((planes,)),
            dma((chunks, planes)), dma((chunks, planes)),
            dma((chunks, group)), dma((chunks, group)),
            dma((chunks,)),
        ],
        compiler_params=pltpu.CompilerParams(
            collective_id=0, has_side_effects=True, vmem_limit_bytes=60 * 2**20
        ),
        cost_estimate=pl.CostEstimate(
            flops=8 * rows * heads * dim * dim,
            bytes_accessed=8 * rows * heads * dim,
            transcendentals=0,
        ),
    )(queries, keys, values, decay_log.T)
    return normalize(mixed, scale, out_gain)


def solution(mesh):
    return jax.shard_map(
        functools.partial(shards, mesh.shape["ctx"], mesh.shape["head"]),
        mesh=mesh,
        in_specs=(
            P(("ctx", "head"), None, None),
            P(("ctx", "head"), None, None),
            P(("ctx", "head"), None, None),
            P(("ctx", "head"), None),
            P(),
        ),
        out_specs=P(("ctx", "head"), None, None),
        check_vma=False,
    )
```

```python
import functools

import jax
import jax.numpy as jnp
from jax import lax
from jax.experimental import pallas as pl
from jax.experimental.pallas import tpu as pltpu
from jax.sharding import PartitionSpec as P

F32, BF16 = jnp.float32, jnp.bfloat16
MESH = pl.DeviceIdType.MESH
TILE = 128


def plan(n_ctx, n_head, heads):
    inner = 1
    for option in (2, 4):
        if n_ctx % option == 0 and heads % (option * n_head) == 0:
            inner = option
    group = inner * n_head
    per_owner = heads // group
    chunks = 1
    for option in (2, 4):
        if per_owner % option == 0 and (heads // option) % 16 == 0:
            chunks = option
    return inner, group, per_owner, chunks


def silu(x):
    half = 0.5 * x
    return half + half * jnp.tanh(half)


def kernel(
    n_ctx, n_head, q_hbm, k_hbm, v_hbm, dec_ref, mix_hbm,
    q_in, k_in, v_in, tmp_a, tmp_b, q_hm, k_hm, v_hm, cum_b, cum_t, end_b, intra,
    ends, ends_in, s_out, s_in, pre, tot_out, tot_in, t_out, t_in, come_x, i_out, i_in,
    in_sem, e_send, e_recv, s_send, s_recv, d_send, d_recv, t_send, t_recv, i_send, i_recv, o_sem,
):
    rows, heads, dim = q_hbm.shape
    inner, group, per_owner, chunks = plan(n_ctx, n_head, heads)
    width = heads // chunks
    hc = per_owner // chunks
    planes = n_ctx // inner
    ctx, head = lax.axis_index("ctx"), lax.axis_index("head")
    plane = ctx // inner
    place = ctx % inner
    me = place * n_head + head

    def device(peer):
        return (plane * inner + peer // n_head, peer % n_head)

    def peer_at(step):
        return lax.rem(me + step, group)

    def load(source, held, at, c):
        return pltpu.make_async_copy(
            source.at[:, pl.ds(c * width, width), :], held.at[c], in_sem.at[at, c]
        )

    load(k_hbm, k_in, 0, 0).start()
    load(v_hbm, v_in, 1, 0).start()

    barrier = pltpu.get_barrier_semaphore()

    def greet(step, carry):
        pl.semaphore_signal(barrier, inc=1, device_id=device(peer_at(step)), device_id_type=MESH)
        return carry

    lax.fori_loop(1, group, greet, 0)

    def greet_plane(step, carry):
        other = lax.rem(plane + step, planes)
        pl.semaphore_signal(
            barrier, inc=1, device_id=(other * inner + place, head), device_id_type=MESH
        )
        return carry

    lax.fori_loop(1, planes, greet_plane, 0)

    decays = dec_ref[...]
    t_at = lax.broadcasted_iota(jnp.int32, (rows, rows), 0)
    s_at = lax.broadcasted_iota(jnp.int32, (rows, rows), 1)
    lower = jnp.where(s_at <= t_at, 1.0, 0.0).astype(BF16)
    upper = jnp.where(t_at <= s_at, 1.0, 0.0).astype(BF16)
    over_rows = (((0,), (0,)), ((), ()))
    cum_t[...] = jnp.dot(decays, upper, preferred_element_type=F32)
    end_b[...] = jnp.dot(decays, jnp.ones((rows, dim), BF16), preferred_element_type=F32)
    for o in range(group):
        for c in range(chunks):
            at = c * width + o * hc
            ends[o, c * hc : (c + 1) * hc, :] = end_b[at : at + hc, :]
    some = 8
    h_at = lax.broadcasted_iota(jnp.int32, (heads, some * dim), 0)
    l_at = lax.broadcasted_iota(jnp.int32, (heads, some * dim), 1) // dim

    def spread(g, carry):
        pick = jnp.where(h_at == l_at + g * some, 1.0, 0.0).astype(BF16)
        wide = lax.dot_general(
            decays, pick, over_rows, preferred_element_type=F32
        ).astype(BF16)
        summed = jnp.dot(lower, wide, preferred_element_type=F32)
        for i in range(some):
            cum_b[g * some + i] = summed[:, i * dim : (i + 1) * dim]
        return carry

    def remote(src, dst, send, recv, to):
        return pltpu.make_async_remote_copy(
            src_ref=src, dst_ref=dst, send_sem=send, recv_sem=recv,
            device_id=to, device_id_type=MESH,
        )

    def end_copy(peer, slot):
        return remote(ends.at[peer], ends_in.at[slot], e_send.at[peer], e_recv.at[slot], device(peer))

    def s_copy(c, peer, slot):
        return remote(
            s_out.at[c, peer], s_in.at[c, slot], s_send.at[c, peer], s_recv.at[c, slot], device(peer)
        )

    def i_copy(c, peer, slot):
        return remote(
            i_out.at[c, peer], i_in.at[c, slot], i_send.at[c, peer], i_recv.at[c, slot], device(peer)
        )

    def at_plane(other):
        return (other * inner + place, head)

    def d_copy(step, slot):
        other = lax.rem(plane + step, planes)
        return remote(tot_out, tot_in.at[slot], d_send.at[step], d_recv.at[slot], at_plane(other))

    def t_copy(c, step, slot):
        other = lax.rem(plane + step, planes)
        return remote(
            t_out.at[c], t_in.at[c, slot], t_send.at[c, step], t_recv.at[c, slot], at_plane(other)
        )

    def each_peer(body):
        def one(step, carry):
            body(peer_at(step))
            return carry

        lax.fori_loop(1, group, one, 0)

    def later_planes(body):
        for step in range(1, planes):
            @pl.when(plane + step < planes)
            def _():
                body(step)

    def earlier_planes(body):
        for p in range(planes - 1):
            @pl.when(p < plane)
            def _():
                body(p)

    step_rows = 16

    def activate(held, c, tmp):
        def some_rows(b, carry):
            x = held[c, pl.ds(b * step_rows, step_rows)].astype(F32)
            tmp[pl.ds(b * step_rows * width, step_rows * width), :] = silu(x).reshape(
                step_rows * width, dim
            )
            return carry

        lax.fori_loop(0, rows // step_rows, some_rows, 0)

    unroll = 4

    def each_head(c, body):
        def one(g, carry):
            for u in range(unroll):
                i = g * unroll + u
                body(i, c * width + i)
            return carry

        lax.fori_loop(0, width // unroll, one, 0)

    owners = max(1, unroll // hc)

    def each_owner(c, first, before, body, after):
        def one(g, carry):
            steps = [first + g * owners + u for u in range(owners)]
            for step in steps:
                before(step, peer_at(step))
            for step in steps:
                for u in range(hc):
                    i = peer_at(step) * hc + u
                    body(i, c * width + i, peer_at(step), u)
            for step in steps:
                after(step, peer_at(step))
            return carry

        lax.fori_loop(0, group // owners, one, 0)

    def nothing(step, peer):
        pass

    def states(c):
        lax.fori_loop(c * width // some, (c + 1) * width // some, spread, 0)
        load(k_hbm, k_in, 0, c).wait()
        load(v_hbm, v_in, 1, c).wait()
        if c + 1 < chunks:
            load(k_hbm, k_in, 0, c + 1).start()
            load(v_hbm, v_in, 1, c + 1).start()
        else:
            for at in range(chunks):
                load(q_hbm, q_in, 2, at).start()
        activate(k_in, c, tmp_a)
        activate(v_in, c, tmp_b)

        def one(i, h, peer, u):
            key = tmp_a[pl.ds(i, rows, stride=width), :].astype(BF16)
            value = tmp_b[pl.ds(i, rows, stride=width), :].astype(BF16)
            k_hm[h] = key
            v_hm[h] = value
            fade = jnp.exp(end_b[pl.ds(h, 1), :] - cum_b[h])
            scaled = (key.astype(F32) * fade).astype(BF16)
            state = lax.dot_general(scaled, value, over_rows, preferred_element_type=F32)
            s_out[c, peer, u * dim : (u + 1) * dim, :] = state.astype(BF16)

        if c == 0:
            pl.semaphore_wait(barrier, group + planes - 2)

        def send(step, peer):
            @pl.when(step < group)
            def _():
                s_copy(c, peer, me).start()

        each_owner(c, 1, nothing, one, send)
        if c == 0:
            each_peer(lambda peer: end_copy(peer, me).start())
            ends_in[me] = ends[me]
        s_in[c, me] = s_out[c, me]

    def inside(c):
        load(q_hbm, q_in, 2, c).wait()
        activate(q_in, c, tmp_a)

        def one(i, h):
            query = tmp_a[pl.ds(i, rows, stride=width), :].astype(BF16)
            q_hm[h] = query
            key, value, cum = k_hm[h], v_hm[h], cum_b[h]
            row = cum_t[pl.ds(h, 1), :]
            outs = []
            for s0 in range(0, rows, TILE):
                w = min(TILE, rows - s0)
                n = rows - s0
                scores = lax.dot_general(
                    query[s0:], key[s0 : s0 + w], (((1,), (1,)), ((), ())),
                    preferred_element_type=F32,
                )
                offset = cum[s0:, :w] - row[:, s0 : s0 + w]
                tt = lax.broadcasted_iota(jnp.int32, (n, w), 0)
                ss = lax.broadcasted_iota(jnp.int32, (n, w), 1)
                weights = scores * jnp.exp(jnp.where(ss <= tt, offset, -1e30))
                outs.append(
                    jnp.dot(
                        weights.astype(BF16), value[s0 : s0 + w], preferred_element_type=F32
                    )
                )
            intra[h] = outs[0]
            for at in range(1, len(outs)):
                intra[h, at * TILE :, :] += outs[at]

        each_head(c, one)

    def join(c):
        if c == 0:
            each_peer(lambda peer: end_copy(peer, peer).wait_recv())
            tot_out[...] = jnp.sum(ends_in[...], axis=0)
            later_planes(lambda step: d_copy(step, plane).start())
        each_peer(lambda peer: s_copy(c, peer, peer).wait_recv())
        for i in range(hc):
            part = pl.ds(i * dim, dim)
            at = c * hc + i
            total = s_in[c, 0, part, :].astype(F32)
            for j in range(1, group):
                pre[c, j, part, :] = total
                fade = jnp.exp(ends_in[j, at : at + 1, :])
                total = fade * total + s_in[c, j, part, :].astype(F32)
            t_out[c, part, :] = total.astype(BF16)
        later_planes(lambda step: t_copy(c, step, plane).start())

    def spread_out(c):
        if c == 0:
            earlier_planes(lambda p: d_copy(1, p).wait_recv())
        earlier_planes(lambda p: t_copy(c, 1, p).wait_recv())
        come_x[...] = jnp.zeros_like(come_x)

        def add(p):
            for i in range(hc):
                part = pl.ds(i * dim, dim)
                at = c * hc + i
                fade = jnp.exp(tot_in[p, at : at + 1, :])
                come_x[part, :] = fade * come_x[part, :] + t_in[c, p, part, :].astype(F32)

        earlier_planes(add)
        fades = [jnp.zeros((1, dim), F32)] * hc
        for j in range(group):
            for i in range(hc):
                part = pl.ds(i * dim, dim)
                at = c * hc + i
                come = come_x[part, :]
                if j > 0:
                    fades[i] = fades[i] + ends_in[j - 1, at : at + 1, :]
                    come = pre[c, j, part, :] + jnp.exp(fades[i]) * come
                i_out[c, j, part, :] = come.astype(BF16)

            @pl.when(j != me)
            def _():
                i_copy(c, j, me).start()

        i_in[c, me] = i_out[c, me]

    def give(c):
        return pltpu.make_async_copy(
            q_in.at[c], mix_hbm.at[:, pl.ds(c * width, width), :], o_sem.at[c]
        )

    def finish(c):
        def arrive(step, peer):
            @pl.when(step > 0)
            def _():
                i_copy(c, peer, peer).wait_recv()

        def one(i, h, peer, u):
            come = i_in[c, peer, u * dim : (u + 1) * dim, :]
            inter = jnp.dot(q_hm[h], come, preferred_element_type=F32)
            mixed = intra[h] + inter * jnp.exp(cum_b[h])
            tmp_a[pl.ds(i, rows, stride=width), :] = mixed

        each_owner(c, 0, arrive, one, nothing)

        def some_rows(b, carry):
            span = step_rows * width
            q_in[c, pl.ds(b * step_rows, step_rows)] = (
                tmp_a[pl.ds(b * span, span), :].reshape(step_rows, width, dim).astype(BF16)
            )
            return carry

        lax.fori_loop(0, rows // step_rows, some_rows, 0)
        give(c).start()

    for c in range(chunks):
        states(c)
    for c in range(chunks):
        join(c)
        inside(c)
        if c > 0:
            spread_out(c - 1)
    spread_out(chunks - 1)
    for c in range(chunks):
        finish(c)

    each_peer(lambda peer: end_copy(peer, me).wait_send())
    later_planes(lambda step: d_copy(step, plane).wait_send())
    for c in range(chunks):
        each_peer(lambda peer: s_copy(c, peer, me).wait_send())
        each_peer(lambda peer: i_copy(c, peer, me).wait_send())
        later_planes(lambda step: t_copy(c, step, plane).wait_send())
        give(c).wait()


def norm_kernel(mixed_ref, gain_ref, out_ref):
    values = mixed_ref[...].astype(F32)
    squares = jnp.sum(jnp.sum(values * values, axis=1, keepdims=True), axis=2, keepdims=True)
    meansq = squares * (1.0 / (values.shape[1] * values.shape[2]))
    out_ref[...] = (values * lax.rsqrt(meansq + 1e-06) * gain_ref[...][None]).astype(BF16)


def normalize(mixed, out_gain):
    rows, heads, dim = mixed.shape
    block = 32 if rows % 32 == 0 else 16
    spec = pl.BlockSpec((block, heads, dim), lambda i: (i, 0, 0))
    return pl.pallas_call(
        norm_kernel,
        out_shape=jax.ShapeDtypeStruct(mixed.shape, BF16),
        grid=(rows // block,),
        in_specs=[spec, pl.BlockSpec((heads, dim), lambda i: (0, 0))],
        out_specs=spec,
    )(mixed, out_gain)


def shards(n_ctx, n_head, queries, keys, values, decay_log, out_gain):
    rows, heads, dim = queries.shape
    inner, group, per_owner, chunks = plan(n_ctx, n_head, heads)
    width, hc = heads // chunks, per_owner // chunks
    held = pltpu.VMEM((chunks, rows, width, dim), BF16)
    major = pltpu.VMEM((heads, rows, dim), BF16)
    block = (hc * dim, dim)
    dma = pltpu.SemaphoreType.DMA
    planes = n_ctx // inner
    tile = (max(8, per_owner), dim)
    mixed = pl.pallas_call(
        functools.partial(kernel, n_ctx, n_head),
        out_shape=jax.ShapeDtypeStruct((rows, heads, dim), BF16),
        in_specs=[pl.BlockSpec(memory_space=pl.ANY)] * 3 + [pl.BlockSpec(memory_space=pltpu.VMEM)],
        out_specs=pl.BlockSpec(memory_space=pl.ANY),
        scratch_shapes=[
            held, held, held,
            pltpu.VMEM((rows * width, dim), F32), pltpu.VMEM((rows * width, dim), F32),
            major, major, major,
            pltpu.VMEM((heads, rows, dim), F32),
            pltpu.VMEM((heads, rows), F32),
            pltpu.VMEM((heads, dim), F32),
            pltpu.VMEM((heads, rows, dim), F32),
            pltpu.VMEM((group,) + tile, F32), pltpu.VMEM((group,) + tile, F32),
            pltpu.VMEM((chunks, group) + block, BF16), pltpu.VMEM((chunks, group) + block, BF16),
            pltpu.VMEM((chunks, group) + block, F32),
            pltpu.VMEM(tile, F32), pltpu.VMEM((planes,) + tile, F32),
            pltpu.VMEM((chunks,) + block, BF16), pltpu.VMEM((chunks, planes) + block, BF16),
            pltpu.VMEM(block, F32),
            pltpu.VMEM((chunks, group) + block, BF16), pltpu.VMEM((chunks, group) + block, BF16),
            dma((3, chunks)),
            dma((group,)), dma((group,)),
            dma((chunks, group)), dma((chunks, group)),
            dma((planes,)), dma((planes,)),
            dma((chunks, planes)), dma((chunks, planes)),
            dma((chunks, group)), dma((chunks, group)),
            dma((chunks,)),
        ],
        compiler_params=pltpu.CompilerParams(
            collective_id=0, has_side_effects=True, vmem_limit_bytes=60 * 2**20
        ),
        cost_estimate=pl.CostEstimate(
            flops=8 * rows * heads * dim * dim,
            bytes_accessed=8 * rows * heads * dim,
            transcendentals=0,
        ),
    )(queries, keys, values, decay_log.T)
    return normalize(mixed, out_gain)


def solution(mesh):
    return jax.shard_map(
        functools.partial(shards, mesh.shape["ctx"], mesh.shape["head"]),
        mesh=mesh,
        in_specs=(
            P(("ctx", "head"), None, None),
            P(("ctx", "head"), None, None),
            P(("ctx", "head"), None, None),
            P(("ctx", "head"), None),
            P(),
        ),
        out_specs=P(("ctx", "head"), None, None),
        check_vma=False,
    )
```

```python
import functools

import jax
import jax.numpy as jnp
from jax import lax
from jax.experimental import pallas as pl
from jax.experimental.pallas import tpu as pltpu
from jax.sharding import PartitionSpec as P

F32, BF16 = jnp.float32, jnp.bfloat16
MESH = pl.DeviceIdType.MESH
TILE = 128


def plan(n_ctx, n_head, heads):
    inner = 1
    for option in (2, 4):
        if n_ctx % option == 0 and heads % (option * n_head) == 0:
            inner = option
    group = inner * n_head
    per_owner = heads // group
    chunks = 1
    for option in (2, 4):
        if per_owner % option == 0 and (heads // option) % 16 == 0:
            chunks = option
    return inner, group, per_owner, chunks


def silu(x):
    half = 0.5 * x
    return half + half * jnp.tanh(half)


def kernel(
    n_ctx, n_head, q_hbm, k_hbm, v_hbm, dec_ref, mix_ref, scale_ref,
    q_in, k_in, v_in, tmp_a, tmp_b, q_hm, k_hm, v_hm, cum_b, cum_t, end_b, intra,
    ends, ends_in, s_out, s_in, pre, tot_out, tot_in, t_out, t_in, come_x, i_out, i_in, squares,
    in_sem, e_send, e_recv, s_send, s_recv, d_send, d_recv, t_send, t_recv, i_send, i_recv,
):
    rows, heads, dim = q_hbm.shape
    inner, group, per_owner, chunks = plan(n_ctx, n_head, heads)
    width = heads // chunks
    hc = per_owner // chunks
    planes = n_ctx // inner
    ctx, head = lax.axis_index("ctx"), lax.axis_index("head")
    plane = ctx // inner
    place = ctx % inner
    me = place * n_head + head

    def device(peer):
        return (plane * inner + peer // n_head, peer % n_head)

    def peer_at(step):
        return lax.rem(me + step, group)

    def load(source, held, at, c):
        return pltpu.make_async_copy(
            source.at[:, pl.ds(c * width, width), :], held.at[c], in_sem.at[at, c]
        )

    load(k_hbm, k_in, 0, 0).start()
    load(v_hbm, v_in, 1, 0).start()

    barrier = pltpu.get_barrier_semaphore()

    def greet(step, carry):
        pl.semaphore_signal(barrier, inc=1, device_id=device(peer_at(step)), device_id_type=MESH)
        return carry

    lax.fori_loop(1, group, greet, 0)

    def greet_plane(step, carry):
        other = lax.rem(plane + step, planes)
        pl.semaphore_signal(
            barrier, inc=1, device_id=(other * inner + place, head), device_id_type=MESH
        )
        return carry

    lax.fori_loop(1, planes, greet_plane, 0)

    decays = dec_ref[...]
    t_at = lax.broadcasted_iota(jnp.int32, (rows, rows), 0)
    s_at = lax.broadcasted_iota(jnp.int32, (rows, rows), 1)
    lower = jnp.where(s_at <= t_at, 1.0, 0.0).astype(BF16)
    upper = jnp.where(t_at <= s_at, 1.0, 0.0).astype(BF16)
    over_rows = (((0,), (0,)), ((), ()))
    cum_t[...] = jnp.dot(decays, upper, preferred_element_type=F32)
    end_b[...] = jnp.dot(decays, jnp.ones((rows, dim), BF16), preferred_element_type=F32)
    for o in range(group):
        for c in range(chunks):
            at = c * width + o * hc
            ends[o, c * hc : (c + 1) * hc, :] = end_b[at : at + hc, :]
    squares[...] = jnp.zeros_like(squares)
    some = 8
    h_at = lax.broadcasted_iota(jnp.int32, (heads, some * dim), 0)
    l_at = lax.broadcasted_iota(jnp.int32, (heads, some * dim), 1) // dim

    def spread(g, carry):
        pick = jnp.where(h_at == l_at + g * some, 1.0, 0.0).astype(BF16)
        wide = lax.dot_general(
            decays, pick, over_rows, preferred_element_type=F32
        ).astype(BF16)
        summed = jnp.dot(lower, wide, preferred_element_type=F32)
        for i in range(some):
            cum_b[g * some + i] = summed[:, i * dim : (i + 1) * dim]
        return carry

    def remote(src, dst, send, recv, to):
        return pltpu.make_async_remote_copy(
            src_ref=src, dst_ref=dst, send_sem=send, recv_sem=recv,
            device_id=to, device_id_type=MESH,
        )

    def end_copy(peer, slot):
        return remote(ends.at[peer], ends_in.at[slot], e_send.at[peer], e_recv.at[slot], device(peer))

    def s_copy(c, peer, slot):
        return remote(
            s_out.at[c, peer], s_in.at[c, slot], s_send.at[c, peer], s_recv.at[c, slot], device(peer)
        )

    def i_copy(c, peer, slot):
        return remote(
            i_out.at[c, peer], i_in.at[c, slot], i_send.at[c, peer], i_recv.at[c, slot], device(peer)
        )

    def at_plane(other):
        return (other * inner + place, head)

    def d_copy(step, slot):
        other = lax.rem(plane + step, planes)
        return remote(tot_out, tot_in.at[slot], d_send.at[step], d_recv.at[slot], at_plane(other))

    def t_copy(c, step, slot):
        other = lax.rem(plane + step, planes)
        return remote(
            t_out.at[c], t_in.at[c, slot], t_send.at[c, step], t_recv.at[c, slot], at_plane(other)
        )

    def each_peer(body):
        def one(step, carry):
            body(peer_at(step))
            return carry

        lax.fori_loop(1, group, one, 0)

    def later_planes(body):
        for step in range(1, planes):
            @pl.when(plane + step < planes)
            def _():
                body(step)

    def earlier_planes(body):
        for p in range(planes - 1):
            @pl.when(p < plane)
            def _():
                body(p)

    step_rows = 16

    def activate(held, c, tmp):
        def some_rows(b, carry):
            x = held[c, pl.ds(b * step_rows, step_rows)].astype(F32)
            tmp[pl.ds(b * step_rows * width, step_rows * width), :] = silu(x).reshape(
                step_rows * width, dim
            )
            return carry

        lax.fori_loop(0, rows // step_rows, some_rows, 0)

    unroll = 4

    def each_head(c, body):
        def one(g, carry):
            for u in range(unroll):
                i = g * unroll + u
                body(i, c * width + i)
            return carry

        lax.fori_loop(0, width // unroll, one, 0)

    owners = max(1, unroll // hc)

    def each_owner(c, first, before, body, after):
        def one(g, carry):
            steps = [first + g * owners + u for u in range(owners)]
            for step in steps:
                before(step, peer_at(step))
            for step in steps:
                for u in range(hc):
                    i = peer_at(step) * hc + u
                    body(i, c * width + i, peer_at(step), u)
            for step in steps:
                after(step, peer_at(step))
            return carry

        lax.fori_loop(0, group // owners, one, 0)

    def nothing(step, peer):
        pass

    def states(c):
        lax.fori_loop(c * width // some, (c + 1) * width // some, spread, 0)
        load(k_hbm, k_in, 0, c).wait()
        load(v_hbm, v_in, 1, c).wait()
        if c + 1 < chunks:
            load(k_hbm, k_in, 0, c + 1).start()
            load(v_hbm, v_in, 1, c + 1).start()
        else:
            for at in range(chunks):
                load(q_hbm, q_in, 2, at).start()
        activate(k_in, c, tmp_a)
        activate(v_in, c, tmp_b)

        def one(i, h, peer, u):
            key = tmp_a[pl.ds(i, rows, stride=width), :].astype(BF16)
            value = tmp_b[pl.ds(i, rows, stride=width), :].astype(BF16)
            k_hm[h] = key
            v_hm[h] = value
            fade = jnp.exp(end_b[pl.ds(h, 1), :] - cum_b[h])
            scaled = (key.astype(F32) * fade).astype(BF16)
            state = lax.dot_general(scaled, value, over_rows, preferred_element_type=F32)
            s_out[c, peer, u * dim : (u + 1) * dim, :] = state.astype(BF16)

        if c == 0:
            pl.semaphore_wait(barrier, group + planes - 2)

        def send(step, peer):
            @pl.when(step < group)
            def _():
                s_copy(c, peer, me).start()

        each_owner(c, 1, nothing, one, send)
        if c == 0:
            each_peer(lambda peer: end_copy(peer, me).start())
            ends_in[me] = ends[me]
        s_in[c, me] = s_out[c, me]

    def inside(c):
        load(q_hbm, q_in, 2, c).wait()
        activate(q_in, c, tmp_a)

        def one(i, h):
            query = tmp_a[pl.ds(i, rows, stride=width), :].astype(BF16)
            q_hm[h] = query
            key, value, cum = k_hm[h], v_hm[h], cum_b[h]
            row = cum_t[pl.ds(h, 1), :]
            outs = []
            for s0 in range(0, rows, TILE):
                w = min(TILE, rows - s0)
                n = rows - s0
                scores = lax.dot_general(
                    query[s0:], key[s0 : s0 + w], (((1,), (1,)), ((), ())),
                    preferred_element_type=F32,
                )
                offset = cum[s0:, :w] - row[:, s0 : s0 + w]
                tt = lax.broadcasted_iota(jnp.int32, (n, w), 0)
                ss = lax.broadcasted_iota(jnp.int32, (n, w), 1)
                weights = scores * jnp.exp(jnp.where(ss <= tt, offset, -1e30))
                outs.append(
                    jnp.dot(
                        weights.astype(BF16), value[s0 : s0 + w], preferred_element_type=F32
                    )
                )
            intra[h] = outs[0]
            for at in range(1, len(outs)):
                intra[h, at * TILE :, :] += outs[at]

        each_head(c, one)

    def join(c):
        if c == 0:
            each_peer(lambda peer: end_copy(peer, peer).wait_recv())
            tot_out[...] = jnp.sum(ends_in[...], axis=0)
            later_planes(lambda step: d_copy(step, plane).start())
        each_peer(lambda peer: s_copy(c, peer, peer).wait_recv())
        for i in range(hc):
            part = pl.ds(i * dim, dim)
            at = c * hc + i
            total = s_in[c, 0, part, :].astype(F32)
            for j in range(1, group):
                pre[c, j, part, :] = total
                fade = jnp.exp(ends_in[j, at : at + 1, :])
                total = fade * total + s_in[c, j, part, :].astype(F32)
            t_out[c, part, :] = total.astype(BF16)
        later_planes(lambda step: t_copy(c, step, plane).start())

    def spread_out(c):
        if c == 0:
            earlier_planes(lambda p: d_copy(1, p).wait_recv())
        earlier_planes(lambda p: t_copy(c, 1, p).wait_recv())
        come_x[...] = jnp.zeros_like(come_x)

        def add(p):
            for i in range(hc):
                part = pl.ds(i * dim, dim)
                at = c * hc + i
                fade = jnp.exp(tot_in[p, at : at + 1, :])
                come_x[part, :] = fade * come_x[part, :] + t_in[c, p, part, :].astype(F32)

        earlier_planes(add)
        fades = [jnp.zeros((1, dim), F32)] * hc
        for j in range(group):
            for i in range(hc):
                part = pl.ds(i * dim, dim)
                at = c * hc + i
                come = come_x[part, :]
                if j > 0:
                    fades[i] = fades[i] + ends_in[j - 1, at : at + 1, :]
                    come = pre[c, j, part, :] + jnp.exp(fades[i]) * come
                i_out[c, j, part, :] = come.astype(BF16)

            @pl.when(j != me)
            def _():
                i_copy(c, j, me).start()

        i_in[c, me] = i_out[c, me]

    def finish(c):
        def arrive(step, peer):
            @pl.when(step > 0)
            def _():
                i_copy(c, peer, peer).wait_recv()

        def one(i, h, peer, u):
            come = i_in[c, peer, u * dim : (u + 1) * dim, :]
            inter = jnp.dot(q_hm[h], come, preferred_element_type=F32)
            mixed = (intra[h] + inter * jnp.exp(cum_b[h])).astype(BF16).astype(F32)
            squares[...] += mixed * mixed
            tmp_a[pl.ds(i, rows, stride=width), :] = mixed

        each_owner(c, 0, arrive, one, nothing)

        def some_rows(b, carry):
            span = step_rows * width
            mix_ref[pl.ds(b * step_rows, step_rows), c * width : (c + 1) * width, :] = (
                tmp_a[pl.ds(b * span, span), :].reshape(step_rows, width, dim).astype(BF16)
            )
            return carry

        lax.fori_loop(0, rows // step_rows, some_rows, 0)

    for c in range(chunks):
        states(c)
    for c in range(chunks):
        join(c)
        inside(c)
        if c > 0:
            spread_out(c - 1)
    spread_out(chunks - 1)
    for c in range(chunks):
        finish(c)
    meansq = jnp.sum(squares[...], axis=1, keepdims=True) * (1.0 / (heads * dim))
    scale_ref[...] = jnp.broadcast_to(lax.rsqrt(meansq + 1e-06), scale_ref.shape)

    each_peer(lambda peer: end_copy(peer, me).wait_send())
    later_planes(lambda step: d_copy(step, plane).wait_send())
    for c in range(chunks):
        each_peer(lambda peer: s_copy(c, peer, me).wait_send())
        each_peer(lambda peer: i_copy(c, peer, me).wait_send())
        later_planes(lambda step: t_copy(c, step, plane).wait_send())


def normalize(mixed, scale, out_gain):
    return (mixed.astype(F32) * scale[:, None, :] * out_gain[None]).astype(BF16)


def shards(n_ctx, n_head, queries, keys, values, decay_log, out_gain):
    rows, heads, dim = queries.shape
    inner, group, per_owner, chunks = plan(n_ctx, n_head, heads)
    width, hc = heads // chunks, per_owner // chunks
    held = pltpu.VMEM((chunks, rows, width, dim), BF16)
    major = pltpu.VMEM((heads, rows, dim), BF16)
    block = (hc * dim, dim)
    dma = pltpu.SemaphoreType.DMA
    planes = n_ctx // inner
    tile = (max(8, per_owner), dim)
    mixed, scale = pl.pallas_call(
        functools.partial(kernel, n_ctx, n_head),
        out_shape=(
            jax.ShapeDtypeStruct((rows, heads, dim), BF16),
            jax.ShapeDtypeStruct((rows, dim), F32),
        ),
        in_specs=[pl.BlockSpec(memory_space=pl.ANY)] * 3 + [pl.BlockSpec(memory_space=pltpu.VMEM)],
        out_specs=(pl.BlockSpec(memory_space=pltpu.VMEM),) * 2,
        scratch_shapes=[
            held, held, held,
            pltpu.VMEM((rows * width, dim), F32), pltpu.VMEM((rows * width, dim), F32),
            major, major, major,
            pltpu.VMEM((heads, rows, dim), F32),
            pltpu.VMEM((heads, rows), F32),
            pltpu.VMEM((heads, dim), F32),
            pltpu.VMEM((heads, rows, dim), F32),
            pltpu.VMEM((group,) + tile, F32), pltpu.VMEM((group,) + tile, F32),
            pltpu.VMEM((chunks, group) + block, BF16), pltpu.VMEM((chunks, group) + block, BF16),
            pltpu.VMEM((chunks, group) + block, F32),
            pltpu.VMEM(tile, F32), pltpu.VMEM((planes,) + tile, F32),
            pltpu.VMEM((chunks,) + block, BF16), pltpu.VMEM((chunks, planes) + block, BF16),
            pltpu.VMEM(block, F32),
            pltpu.VMEM((chunks, group) + block, BF16), pltpu.VMEM((chunks, group) + block, BF16),
            pltpu.VMEM((rows, dim), F32),
            dma((3, chunks)),
            dma((group,)), dma((group,)),
            dma((chunks, group)), dma((chunks, group)),
            dma((planes,)), dma((planes,)),
            dma((chunks, planes)), dma((chunks, planes)),
            dma((chunks, group)), dma((chunks, group)),
        ],
        compiler_params=pltpu.CompilerParams(
            collective_id=0, has_side_effects=True, vmem_limit_bytes=50 * 2**20
        ),
        cost_estimate=pl.CostEstimate(
            flops=8 * rows * heads * dim * dim,
            bytes_accessed=8 * rows * heads * dim,
            transcendentals=0,
        ),
    )(queries, keys, values, decay_log.T)
    return normalize(mixed, scale, out_gain)


def solution(mesh):
    return jax.shard_map(
        functools.partial(shards, mesh.shape["ctx"], mesh.shape["head"]),
        mesh=mesh,
        in_specs=(
            P(("ctx", "head"), None, None),
            P(("ctx", "head"), None, None),
            P(("ctx", "head"), None, None),
            P(("ctx", "head"), None),
            P(),
        ),
        out_specs=P(("ctx", "head"), None, None),
        check_vma=False,
    )
```

```python
import functools

import jax
import jax.numpy as jnp
from jax import lax
from jax.experimental import pallas as pl
from jax.experimental.pallas import tpu as pltpu
from jax.sharding import PartitionSpec as P

F32, BF16 = jnp.float32, jnp.bfloat16
MESH = pl.DeviceIdType.MESH
TILE = 128


def plan(n_ctx, n_head, heads):
    inner = 1
    for option in (2, 4):
        if n_ctx % option == 0 and heads % (option * n_head) == 0:
            inner = option
    group = inner * n_head
    per_owner = heads // group
    chunks = 1
    for option in (2, 4):
        if per_owner % option == 0 and (heads // option) % 16 == 0:
            chunks = option
    return inner, group, per_owner, chunks


def silu(x):
    half = 0.5 * x
    return half + half * jnp.tanh(half)


def kernel(
    n_ctx, n_head, q_hbm, k_hbm, v_hbm, dec_ref, mix_ref, scale_ref,
    q_in, k_in, v_in, tmp_a, tmp_b, q_hm, k_hm, v_hm, cum_b, cum_t, end_b, intra,
    ends, ends_in, s_out, s_in, pre, tot_out, tot_in, t_out, t_in, come_x, i_out, i_in, squares,
    in_sem, e_send, e_recv, s_send, s_recv, d_send, d_recv, t_send, t_recv, i_send, i_recv,
):
    rows, heads, dim = q_hbm.shape
    inner, group, per_owner, chunks = plan(n_ctx, n_head, heads)
    width = heads // chunks
    hc = per_owner // chunks
    planes = n_ctx // inner
    ctx, head = lax.axis_index("ctx"), lax.axis_index("head")
    plane = ctx // inner
    place = ctx % inner
    me = place * n_head + head

    def device(peer):
        return (plane * inner + peer // n_head, peer % n_head)

    def peer_at(step):
        return lax.rem(me + step, group)

    def load(source, held, at, c):
        return pltpu.make_async_copy(
            source.at[:, pl.ds(c * width, width), :], held.at[c], in_sem.at[at, c]
        )

    load(k_hbm, k_in, 0, 0).start()
    load(v_hbm, v_in, 1, 0).start()

    barrier = pltpu.get_barrier_semaphore()

    def greet(step, carry):
        pl.semaphore_signal(barrier, inc=1, device_id=device(peer_at(step)), device_id_type=MESH)
        return carry

    lax.fori_loop(1, group, greet, 0)

    def greet_plane(step, carry):
        other = lax.rem(plane + step, planes)
        pl.semaphore_signal(
            barrier, inc=1, device_id=(other * inner + place, head), device_id_type=MESH
        )
        return carry

    lax.fori_loop(1, planes, greet_plane, 0)

    decays = dec_ref[...]
    t_at = lax.broadcasted_iota(jnp.int32, (rows, rows), 0)
    s_at = lax.broadcasted_iota(jnp.int32, (rows, rows), 1)
    lower = jnp.where(s_at <= t_at, 1.0, 0.0).astype(BF16)
    upper = jnp.where(t_at <= s_at, 1.0, 0.0).astype(BF16)
    over_rows = (((0,), (0,)), ((), ()))
    cum_t[...] = jnp.dot(decays, upper, preferred_element_type=F32)
    end_b[...] = jnp.dot(decays, jnp.ones((rows, dim), BF16), preferred_element_type=F32)
    for o in range(group):
        for c in range(chunks):
            at = c * width + o * hc
            ends[o, c * hc : (c + 1) * hc, :] = end_b[at : at + hc, :]
    squares[...] = jnp.zeros_like(squares)
    some = 8
    h_at = lax.broadcasted_iota(jnp.int32, (heads, some * dim), 0)
    l_at = lax.broadcasted_iota(jnp.int32, (heads, some * dim), 1) // dim

    def spread(g, carry):
        pick = jnp.where(h_at == l_at + g * some, 1.0, 0.0).astype(BF16)
        wide = lax.dot_general(
            decays, pick, over_rows, preferred_element_type=F32
        ).astype(BF16)
        summed = jnp.dot(lower, wide, preferred_element_type=F32)
        for i in range(some):
            cum_b[g * some + i] = summed[:, i * dim : (i + 1) * dim]
        return carry

    def remote(src, dst, send, recv, to):
        return pltpu.make_async_remote_copy(
            src_ref=src, dst_ref=dst, send_sem=send, recv_sem=recv,
            device_id=to, device_id_type=MESH,
        )

    def end_copy(peer, slot):
        return remote(ends.at[peer], ends_in.at[slot], e_send.at[peer], e_recv.at[slot], device(peer))

    def s_copy(c, peer, slot):
        return remote(
            s_out.at[c, peer], s_in.at[c, slot], s_send.at[c, peer], s_recv.at[c, slot], device(peer)
        )

    def i_copy(c, peer, slot):
        return remote(
            i_out.at[c, peer], i_in.at[c, slot], i_send.at[c, peer], i_recv.at[c, slot], device(peer)
        )

    def at_plane(other):
        return (other * inner + place, head)

    def d_copy(step, slot):
        other = lax.rem(plane + step, planes)
        return remote(tot_out, tot_in.at[slot], d_send.at[step], d_recv.at[slot], at_plane(other))

    def t_copy(c, step, slot):
        other = lax.rem(plane + step, planes)
        return remote(
            t_out.at[c], t_in.at[c, slot], t_send.at[c, step], t_recv.at[c, slot], at_plane(other)
        )

    def each_peer(body):
        def one(step, carry):
            body(peer_at(step))
            return carry

        lax.fori_loop(1, group, one, 0)

    def later_planes(body):
        for step in range(1, planes):
            @pl.when(plane + step < planes)
            def _():
                body(step)

    def earlier_planes(body):
        for p in range(planes - 1):
            @pl.when(p < plane)
            def _():
                body(p)

    step_rows = 16
    pitch = width + 1

    def activate(held, c, tmp):
        def some_rows(b, carry):
            x = silu(held[c, pl.ds(b * step_rows, step_rows)].astype(F32))
            base = pl.multiple_of(b * (step_rows * pitch), step_rows)
            for t in range(step_rows):
                tmp[pl.ds(base + t * pitch, width), :] = x[t]
            return carry

        lax.fori_loop(0, rows // step_rows, some_rows, 0)

    unroll = 4

    def each_head(c, body):
        def one(g, carry):
            for u in range(unroll):
                i = g * unroll + u
                body(i, c * width + i)
            return carry

        lax.fori_loop(0, width // unroll, one, 0)

    owners = max(1, unroll // hc)

    def each_owner(c, first, before, body, after):
        def one(g, carry):
            steps = [first + g * owners + u for u in range(owners)]
            for step in steps:
                before(step, peer_at(step))
            for step in steps:
                for u in range(hc):
                    i = peer_at(step) * hc + u
                    body(i, c * width + i, peer_at(step), u)
            for step in steps:
                after(step, peer_at(step))
            return carry

        lax.fori_loop(0, group // owners, one, 0)

    def nothing(step, peer):
        pass

    def states(c):
        lax.fori_loop(c * width // some, (c + 1) * width // some, spread, 0)
        load(k_hbm, k_in, 0, c).wait()
        load(v_hbm, v_in, 1, c).wait()
        if c + 1 < chunks:
            load(k_hbm, k_in, 0, c + 1).start()
            load(v_hbm, v_in, 1, c + 1).start()
        else:
            for at in range(chunks):
                load(q_hbm, q_in, 2, at).start()
        activate(k_in, c, tmp_a)
        activate(v_in, c, tmp_b)

        def one(i, h, peer, u):
            key = tmp_a[pl.ds(i, rows, stride=pitch), :].astype(BF16)
            value = tmp_b[pl.ds(i, rows, stride=pitch), :].astype(BF16)
            k_hm[h] = key
            v_hm[h] = value
            fade = jnp.exp(end_b[pl.ds(h, 1), :] - cum_b[h])
            scaled = (key.astype(F32) * fade).astype(BF16)
            state = lax.dot_general(scaled, value, over_rows, preferred_element_type=F32)
            s_out[c, peer, u * dim : (u + 1) * dim, :] = state.astype(BF16)

        if c == 0:
            pl.semaphore_wait(barrier, group + planes - 2)

        def send(step, peer):
            @pl.when(step < group)
            def _():
                s_copy(c, peer, me).start()

        each_owner(c, 1, nothing, one, send)
        if c == 0:
            each_peer(lambda peer: end_copy(peer, me).start())
            ends_in[me] = ends[me]
        s_in[c, me] = s_out[c, me]

    def inside(c):
        load(q_hbm, q_in, 2, c).wait()
        activate(q_in, c, tmp_a)

        def one(i, h):
            query = tmp_a[pl.ds(i, rows, stride=pitch), :].astype(BF16)
            q_hm[h] = query
            key, value, cum = k_hm[h], v_hm[h], cum_b[h]
            row = cum_t[pl.ds(h, 1), :]
            outs = []
            for s0 in range(0, rows, TILE):
                w = min(TILE, rows - s0)
                n = rows - s0
                scores = lax.dot_general(
                    query[s0:], key[s0 : s0 + w], (((1,), (1,)), ((), ())),
                    preferred_element_type=F32,
                )
                offset = cum[s0:, :w] - row[:, s0 : s0 + w]
                tt = lax.broadcasted_iota(jnp.int32, (n, w), 0)
                ss = lax.broadcasted_iota(jnp.int32, (n, w), 1)
                weights = scores * jnp.exp(jnp.where(ss <= tt, offset, -1e30))
                outs.append(
                    jnp.dot(
                        weights.astype(BF16), value[s0 : s0 + w], preferred_element_type=F32
                    )
                )
            intra[h] = outs[0]
            for at in range(1, len(outs)):
                intra[h, at * TILE :, :] += outs[at]

        each_head(c, one)

    def join(c):
        if c == 0:
            each_peer(lambda peer: end_copy(peer, peer).wait_recv())
            tot_out[...] = jnp.sum(ends_in[...], axis=0)
            later_planes(lambda step: d_copy(step, plane).start())
        each_peer(lambda peer: s_copy(c, peer, peer).wait_recv())
        for i in range(hc):
            part = pl.ds(i * dim, dim)
            at = c * hc + i
            total = s_in[c, 0, part, :].astype(F32)
            for j in range(1, group):
                pre[c, j, part, :] = total
                fade = jnp.exp(ends_in[j, at : at + 1, :])
                total = fade * total + s_in[c, j, part, :].astype(F32)
            t_out[c, part, :] = total.astype(BF16)
        later_planes(lambda step: t_copy(c, step, plane).start())

    def spread_out(c):
        if c == 0:
            earlier_planes(lambda p: d_copy(1, p).wait_recv())
        earlier_planes(lambda p: t_copy(c, 1, p).wait_recv())
        come_x[...] = jnp.zeros_like(come_x)

        def add(p):
            for i in range(hc):
                part = pl.ds(i * dim, dim)
                at = c * hc + i
                fade = jnp.exp(tot_in[p, at : at + 1, :])
                come_x[part, :] = fade * come_x[part, :] + t_in[c, p, part, :].astype(F32)

        earlier_planes(add)
        fades = [jnp.zeros((1, dim), F32)] * hc
        for j in range(group):
            for i in range(hc):
                part = pl.ds(i * dim, dim)
                at = c * hc + i
                come = come_x[part, :]
                if j > 0:
                    fades[i] = fades[i] + ends_in[j - 1, at : at + 1, :]
                    come = pre[c, j, part, :] + jnp.exp(fades[i]) * come
                i_out[c, j, part, :] = come.astype(BF16)

            @pl.when(j != me)
            def _():
                i_copy(c, j, me).start()

        i_in[c, me] = i_out[c, me]

    def finish(c):
        def arrive(step, peer):
            @pl.when(step > 0)
            def _():
                i_copy(c, peer, peer).wait_recv()

        def one(i, h, peer, u):
            come = i_in[c, peer, u * dim : (u + 1) * dim, :]
            inter = jnp.dot(q_hm[h], come, preferred_element_type=F32)
            mixed = (intra[h] + inter * jnp.exp(cum_b[h])).astype(BF16).astype(F32)
            squares[...] += mixed * mixed
            tmp_a[pl.ds(i, rows, stride=pitch), :] = mixed

        each_owner(c, 0, arrive, one, nothing)

        def some_rows(b, carry):
            base = pl.multiple_of(b * (step_rows * pitch), step_rows)
            for t in range(step_rows):
                mix_ref[b * step_rows + t, c * width : (c + 1) * width, :] = tmp_a[
                    pl.ds(base + t * pitch, width), :
                ].astype(BF16)
            return carry

        lax.fori_loop(0, rows // step_rows, some_rows, 0)

    for c in range(chunks):
        states(c)
    for c in range(chunks):
        join(c)
        inside(c)
        if c > 0:
            spread_out(c - 1)
    spread_out(chunks - 1)
    for c in range(chunks):
        finish(c)
    meansq = jnp.sum(squares[...], axis=1, keepdims=True) * (1.0 / (heads * dim))
    scale_ref[...] = jnp.broadcast_to(lax.rsqrt(meansq + 1e-06), scale_ref.shape)

    each_peer(lambda peer: end_copy(peer, me).wait_send())
    later_planes(lambda step: d_copy(step, plane).wait_send())
    for c in range(chunks):
        each_peer(lambda peer: s_copy(c, peer, me).wait_send())
        each_peer(lambda peer: i_copy(c, peer, me).wait_send())
        later_planes(lambda step: t_copy(c, step, plane).wait_send())


def normalize(mixed, scale, out_gain):
    return (mixed.astype(F32) * scale[:, None, :] * out_gain[None]).astype(BF16)


def shards(n_ctx, n_head, queries, keys, values, decay_log, out_gain):
    rows, heads, dim = queries.shape
    inner, group, per_owner, chunks = plan(n_ctx, n_head, heads)
    width, hc = heads // chunks, per_owner // chunks
    held = pltpu.VMEM((chunks, rows, width, dim), BF16)
    major = pltpu.VMEM((heads, rows, dim), BF16)
    block = (hc * dim, dim)
    dma = pltpu.SemaphoreType.DMA
    planes = n_ctx // inner
    tile = (max(8, per_owner), dim)
    mixed, scale = pl.pallas_call(
        functools.partial(kernel, n_ctx, n_head),
        out_shape=(
            jax.ShapeDtypeStruct((rows, heads, dim), BF16),
            jax.ShapeDtypeStruct((rows, dim), F32),
        ),
        in_specs=[pl.BlockSpec(memory_space=pl.ANY)] * 3 + [pl.BlockSpec(memory_space=pltpu.VMEM)],
        out_specs=(pl.BlockSpec(memory_space=pltpu.VMEM),) * 2,
        scratch_shapes=[
            held, held, held,
            pltpu.VMEM((rows * (width + 1), dim), F32), pltpu.VMEM((rows * (width + 1), dim), F32),
            major, major, major,
            pltpu.VMEM((heads, rows, dim), F32),
            pltpu.VMEM((heads, rows), F32),
            pltpu.VMEM((heads, dim), F32),
            pltpu.VMEM((heads, rows, dim), F32),
            pltpu.VMEM((group,) + tile, F32), pltpu.VMEM((group,) + tile, F32),
            pltpu.VMEM((chunks, group) + block, BF16), pltpu.VMEM((chunks, group) + block, BF16),
            pltpu.VMEM((chunks, group) + block, F32),
            pltpu.VMEM(tile, F32), pltpu.VMEM((planes,) + tile, F32),
            pltpu.VMEM((chunks,) + block, BF16), pltpu.VMEM((chunks, planes) + block, BF16),
            pltpu.VMEM(block, F32),
            pltpu.VMEM((chunks, group) + block, BF16), pltpu.VMEM((chunks, group) + block, BF16),
            pltpu.VMEM((rows, dim), F32),
            dma((3, chunks)),
            dma((group,)), dma((group,)),
            dma((chunks, group)), dma((chunks, group)),
            dma((planes,)), dma((planes,)),
            dma((chunks, planes)), dma((chunks, planes)),
            dma((chunks, group)), dma((chunks, group)),
        ],
        compiler_params=pltpu.CompilerParams(
            collective_id=0, has_side_effects=True, vmem_limit_bytes=50 * 2**20
        ),
        cost_estimate=pl.CostEstimate(
            flops=8 * rows * heads * dim * dim,
            bytes_accessed=8 * rows * heads * dim,
            transcendentals=0,
        ),
    )(queries, keys, values, decay_log.T)
    return normalize(mixed, scale, out_gain)


def solution(mesh):
    return jax.shard_map(
        functools.partial(shards, mesh.shape["ctx"], mesh.shape["head"]),
        mesh=mesh,
        in_specs=(
            P(("ctx", "head"), None, None),
            P(("ctx", "head"), None, None),
            P(("ctx", "head"), None, None),
            P(("ctx", "head"), None),
            P(),
        ),
        out_specs=P(("ctx", "head"), None, None),
        check_vma=False,
    )
```

```python
import functools

import jax
import jax.numpy as jnp
from jax import lax
from jax.experimental import pallas as pl
from jax.experimental.pallas import tpu as pltpu
from jax.sharding import PartitionSpec as P

F32, BF16 = jnp.float32, jnp.bfloat16
MESH = pl.DeviceIdType.MESH
TILE = 128


def plan(n_ctx, n_head, heads):
    inner = 1
    for option in (2, 4):
        if n_ctx % option == 0 and heads % (option * n_head) == 0:
            inner = option
    group = inner * n_head
    per_owner = heads // group
    chunks = 1
    for option in (2, 4):
        if per_owner % option == 0 and (heads // option) % 16 == 0:
            chunks = option
    return inner, group, per_owner, chunks


def silu(x):
    half = 0.5 * x
    return half + half * jnp.tanh(half)


def kernel(
    n_ctx, n_head, q_hbm, k_hbm, v_hbm, dec_ref, mix_ref, scale_ref,
    q_in, k_in, v_in, tmp_a, tmp_b, q_hm, k_hm, v_hm, cum_b, cum_t, end_b, intra,
    ends, ends_in, s_out, s_in, pre, tot_out, tot_in, t_out, t_in, come_x, i_out, i_in, squares,
    in_sem, e_send, e_recv, s_send, s_recv, d_send, d_recv, t_send, t_recv, i_send, i_recv,
):
    rows, heads, dim = q_hbm.shape
    inner, group, per_owner, chunks = plan(n_ctx, n_head, heads)
    width = heads // chunks
    hc = per_owner // chunks
    planes = n_ctx // inner
    ctx, head = lax.axis_index("ctx"), lax.axis_index("head")
    plane = ctx // inner
    place = ctx % inner
    me = place * n_head + head

    def device(peer):
        return (plane * inner + peer // n_head, peer % n_head)

    def peer_at(step):
        return lax.rem(me + step, group)

    def load(source, held, at, c):
        return pltpu.make_async_copy(
            source.at[:, pl.ds(c * width, width), :], held.at[c], in_sem.at[at, c]
        )

    load(k_hbm, k_in, 0, 0).start()
    load(v_hbm, v_in, 1, 0).start()

    barrier = pltpu.get_barrier_semaphore()

    def greet(step, carry):
        pl.semaphore_signal(barrier, inc=1, device_id=device(peer_at(step)), device_id_type=MESH)
        return carry

    lax.fori_loop(1, group, greet, 0)

    def greet_plane(step, carry):
        other = lax.rem(plane + step, planes)
        pl.semaphore_signal(
            barrier, inc=1, device_id=(other * inner + place, head), device_id_type=MESH
        )
        return carry

    lax.fori_loop(1, planes, greet_plane, 0)

    decays = dec_ref[...]
    t_at = lax.broadcasted_iota(jnp.int32, (rows, rows), 0)
    s_at = lax.broadcasted_iota(jnp.int32, (rows, rows), 1)
    lower = jnp.where(s_at <= t_at, 1.0, 0.0).astype(BF16)
    upper = jnp.where(t_at <= s_at, 1.0, 0.0).astype(BF16)
    over_rows = (((0,), (0,)), ((), ()))
    cum_t[...] = jnp.dot(decays, upper, preferred_element_type=F32)
    end_b[...] = jnp.dot(decays, jnp.ones((rows, dim), BF16), preferred_element_type=F32)
    squares[...] = jnp.zeros_like(squares)
    some = 8
    h_at = lax.broadcasted_iota(jnp.int32, (heads, some * dim), 0)
    l_at = lax.broadcasted_iota(jnp.int32, (heads, some * dim), 1) // dim

    def spread(g, carry):
        pick = jnp.where(h_at == l_at + g * some, 1.0, 0.0).astype(BF16)
        wide = lax.dot_general(
            decays, pick, over_rows, preferred_element_type=F32
        ).astype(BF16)
        summed = jnp.dot(lower, wide, preferred_element_type=F32)
        for i in range(some):
            cum_b[g * some + i] = summed[:, i * dim : (i + 1) * dim]
        return carry

    def remote(src, dst, send, recv, to):
        return pltpu.make_async_remote_copy(
            src_ref=src, dst_ref=dst, send_sem=send, recv_sem=recv,
            device_id=to, device_id_type=MESH,
        )

    def end_copy(peer, slot):
        return remote(ends.at[peer], ends_in.at[slot], e_send.at[peer], e_recv.at[slot], device(peer))

    def s_copy(c, peer, slot):
        return remote(
            s_out.at[c, peer], s_in.at[c, slot], s_send.at[c, peer], s_recv.at[c, slot], device(peer)
        )

    def i_copy(c, peer, slot):
        return remote(
            i_out.at[c, peer], i_in.at[c, slot], i_send.at[c, peer], i_recv.at[c, slot], device(peer)
        )

    def at_plane(other):
        return (other * inner + place, head)

    def d_copy(step, slot):
        other = lax.rem(plane + step, planes)
        return remote(tot_out, tot_in.at[slot], d_send.at[step], d_recv.at[slot], at_plane(other))

    def t_copy(c, step, slot):
        other = lax.rem(plane + step, planes)
        return remote(
            t_out.at[c], t_in.at[c, slot], t_send.at[c, step], t_recv.at[c, slot], at_plane(other)
        )

    def each_peer(body):
        def one(step, carry):
            body(peer_at(step))
            return carry

        lax.fori_loop(1, group, one, 0)

    def later_planes(body):
        for step in range(1, planes):
            @pl.when(plane + step < planes)
            def _():
                body(step)

    def earlier_planes(body):
        for p in range(planes - 1):
            @pl.when(p < plane)
            def _():
                body(p)

    step_rows = 16
    pitch = width + 1

    def activate(held, c, tmp):
        def some_rows(b, carry):
            x = silu(held[c, pl.ds(b * step_rows, step_rows)].astype(F32))
            base = pl.multiple_of(b * (step_rows * pitch), step_rows)
            for t in range(step_rows):
                tmp[pl.ds(base + t * pitch, width), :] = x[t]
            return carry

        lax.fori_loop(0, rows // step_rows, some_rows, 0)

    unroll = 8

    def each_head(c, body):
        def one(g, carry):
            for u in range(unroll):
                i = g * unroll + u
                body(i, c * width + i)
            return carry

        lax.fori_loop(0, width // unroll, one, 0)

    owners = max(1, unroll // hc)

    def each_owner(c, first, before, body, after):
        def one(g, carry):
            steps = [first + g * owners + u for u in range(owners)]
            for step in steps:
                before(step, peer_at(step))
            for step in steps:
                for u in range(hc):
                    i = peer_at(step) * hc + u
                    body(i, c * width + i, peer_at(step), u)
            for step in steps:
                after(step, peer_at(step))
            return carry

        lax.fori_loop(0, group // owners, one, 0)

    def nothing(step, peer):
        pass

    def states(c):
        lax.fori_loop(c * width // some, (c + 1) * width // some, spread, 0)
        load(k_hbm, k_in, 0, c).wait()
        load(v_hbm, v_in, 1, c).wait()
        if c + 1 < chunks:
            load(k_hbm, k_in, 0, c + 1).start()
            load(v_hbm, v_in, 1, c + 1).start()
        else:
            for at in range(chunks):
                load(q_hbm, q_in, 2, at).start()
        activate(k_in, c, tmp_a)
        activate(v_in, c, tmp_b)

        def one(i, h, peer, u):
            key = tmp_a[pl.ds(i, rows, stride=pitch), :].astype(BF16)
            value = tmp_b[pl.ds(i, rows, stride=pitch), :].astype(BF16)
            k_hm[h] = key
            v_hm[h] = value
            fade = jnp.exp(end_b[pl.ds(h, 1), :] - cum_b[h])
            scaled = (key.astype(F32) * fade).astype(BF16)
            state = lax.dot_general(scaled, value, over_rows, preferred_element_type=F32)
            s_out[c, peer, u * dim : (u + 1) * dim, :] = state.astype(BF16)

        if c == 0:
            pl.semaphore_wait(barrier, group + planes - 2)

        def send(step, peer):
            @pl.when(step < group)
            def _():
                s_copy(c, peer, me).start()

        each_owner(c, 1, nothing, one, send)
        if c == 0:
            for o in range(group):
                for d in range(chunks):
                    at = d * width + o * hc
                    ends[o, d * hc : (d + 1) * hc, :] = end_b[at : at + hc, :]
            each_peer(lambda peer: end_copy(peer, me).start())
            ends_in[me] = ends[me]
        s_in[c, me] = s_out[c, me]

    def inside(c):
        load(q_hbm, q_in, 2, c).wait()
        activate(q_in, c, tmp_a)

        def one(i, h):
            query = tmp_a[pl.ds(i, rows, stride=pitch), :].astype(BF16)
            q_hm[h] = query
            key, value, cum = k_hm[h], v_hm[h], cum_b[h]
            row = cum_t[pl.ds(h, 1), :]
            outs = []
            for s0 in range(0, rows, TILE):
                w = min(TILE, rows - s0)
                n = rows - s0
                scores = lax.dot_general(
                    query[s0:], key[s0 : s0 + w], (((1,), (1,)), ((), ())),
                    preferred_element_type=F32,
                )
                offset = cum[s0:, :w] - row[:, s0 : s0 + w]
                tt = lax.broadcasted_iota(jnp.int32, (w, w), 0)
                ss = lax.broadcasted_iota(jnp.int32, (w, w), 1)
                fades = jnp.exp(jnp.where(ss <= tt, offset[:w], -1e30))
                if n > w:
                    fades = jnp.concatenate([fades, jnp.exp(offset[w:])], axis=0)
                weights = scores * fades
                outs.append(
                    jnp.dot(
                        weights.astype(BF16), value[s0 : s0 + w], preferred_element_type=F32
                    )
                )
            intra[h] = outs[0]
            for at in range(1, len(outs)):
                intra[h, at * TILE :, :] += outs[at]

        each_head(c, one)

    def join(c):
        if c == 0:
            each_peer(lambda peer: end_copy(peer, peer).wait_recv())
            tot_out[...] = jnp.sum(ends_in[...], axis=0)
            later_planes(lambda step: d_copy(step, plane).start())
        each_peer(lambda peer: s_copy(c, peer, peer).wait_recv())
        for i in range(hc):
            part = pl.ds(i * dim, dim)
            at = c * hc + i
            total = s_in[c, 0, part, :].astype(F32)
            for j in range(1, group):
                pre[c, j, part, :] = total
                fade = jnp.exp(ends_in[j, at : at + 1, :])
                total = fade * total + s_in[c, j, part, :].astype(F32)
            t_out[c, part, :] = total.astype(BF16)
        later_planes(lambda step: t_copy(c, step, plane).start())

    def spread_out(c):
        if c == 0:
            earlier_planes(lambda p: d_copy(1, p).wait_recv())
        earlier_planes(lambda p: t_copy(c, 1, p).wait_recv())
        come_x[...] = jnp.zeros_like(come_x)

        def add(p):
            for i in range(hc):
                part = pl.ds(i * dim, dim)
                at = c * hc + i
                fade = jnp.exp(tot_in[p, at : at + 1, :])
                come_x[part, :] = fade * come_x[part, :] + t_in[c, p, part, :].astype(F32)

        earlier_planes(add)
        fades = [jnp.zeros((1, dim), F32)] * hc
        for j in range(group):
            for i in range(hc):
                part = pl.ds(i * dim, dim)
                at = c * hc + i
                come = come_x[part, :]
                if j > 0:
                    fades[i] = fades[i] + ends_in[j - 1, at : at + 1, :]
                    come = pre[c, j, part, :] + jnp.exp(fades[i]) * come
                i_out[c, j, part, :] = come.astype(BF16)

            @pl.when(j != me)
            def _():
                i_copy(c, j, me).start()

        i_in[c, me] = i_out[c, me]

    def finish(c):
        def arrive(step, peer):
            @pl.when(step > 0)
            def _():
                i_copy(c, peer, peer).wait_recv()

        def one(i, h, peer, u):
            come = i_in[c, peer, u * dim : (u + 1) * dim, :]
            inter = jnp.dot(q_hm[h], come, preferred_element_type=F32)
            mixed = (intra[h] + inter * jnp.exp(cum_b[h])).astype(BF16).astype(F32)
            squares[...] += mixed * mixed
            tmp_a[pl.ds(i, rows, stride=pitch), :] = mixed

        each_owner(c, 0, arrive, one, nothing)

        def some_rows(b, carry):
            base = pl.multiple_of(b * (step_rows * pitch), step_rows)
            for t in range(step_rows):
                mix_ref[b * step_rows + t, c * width : (c + 1) * width, :] = tmp_a[
                    pl.ds(base + t * pitch, width), :
                ].astype(BF16)
            return carry

        lax.fori_loop(0, rows // step_rows, some_rows, 0)

    for c in range(chunks):
        states(c)
    for c in range(chunks):
        join(c)
        inside(c)
        if c > 0:
            spread_out(c - 1)
    spread_out(chunks - 1)
    for c in range(chunks):
        finish(c)
    meansq = jnp.sum(squares[...], axis=1, keepdims=True) * (1.0 / (heads * dim))
    scale_ref[...] = jnp.broadcast_to(lax.rsqrt(meansq + 1e-06), scale_ref.shape)

    each_peer(lambda peer: end_copy(peer, me).wait_send())
    later_planes(lambda step: d_copy(step, plane).wait_send())
    for c in range(chunks):
        each_peer(lambda peer: s_copy(c, peer, me).wait_send())
        each_peer(lambda peer: i_copy(c, peer, me).wait_send())
        later_planes(lambda step: t_copy(c, step, plane).wait_send())


def normalize(mixed, scale, out_gain):
    return (mixed.astype(F32) * scale[:, None, :] * out_gain[None]).astype(BF16)


def shards(n_ctx, n_head, queries, keys, values, decay_log, out_gain):
    rows, heads, dim = queries.shape
    inner, group, per_owner, chunks = plan(n_ctx, n_head, heads)
    width, hc = heads // chunks, per_owner // chunks
    held = pltpu.VMEM((chunks, rows, width, dim), BF16)
    major = pltpu.VMEM((heads, rows, dim), BF16)
    block = (hc * dim, dim)
    dma = pltpu.SemaphoreType.DMA
    planes = n_ctx // inner
    tile = (max(8, per_owner), dim)
    mixed, scale = pl.pallas_call(
        functools.partial(kernel, n_ctx, n_head),
        out_shape=(
            jax.ShapeDtypeStruct((rows, heads, dim), BF16),
            jax.ShapeDtypeStruct((rows, dim), F32),
        ),
        in_specs=[pl.BlockSpec(memory_space=pl.ANY)] * 3 + [pl.BlockSpec(memory_space=pltpu.VMEM)],
        out_specs=(pl.BlockSpec(memory_space=pltpu.VMEM),) * 2,
        scratch_shapes=[
            held, held, held,
            pltpu.VMEM((rows * (width + 1), dim), F32), pltpu.VMEM((rows * (width + 1), dim), F32),
            major, major, major,
            pltpu.VMEM((heads, rows, dim), F32),
            pltpu.VMEM((heads, rows), F32),
            pltpu.VMEM((heads, dim), F32),
            pltpu.VMEM((heads, rows, dim), F32),
            pltpu.VMEM((group,) + tile, F32), pltpu.VMEM((group,) + tile, F32),
            pltpu.VMEM((chunks, group) + block, BF16), pltpu.VMEM((chunks, group) + block, BF16),
            pltpu.VMEM((chunks, group) + block, F32),
            pltpu.VMEM(tile, F32), pltpu.VMEM((planes,) + tile, F32),
            pltpu.VMEM((chunks,) + block, BF16), pltpu.VMEM((chunks, planes) + block, BF16),
            pltpu.VMEM(block, F32),
            pltpu.VMEM((chunks, group) + block, BF16), pltpu.VMEM((chunks, group) + block, BF16),
            pltpu.VMEM((rows, dim), F32),
            dma((3, chunks)),
            dma((group,)), dma((group,)),
            dma((chunks, group)), dma((chunks, group)),
            dma((planes,)), dma((planes,)),
            dma((chunks, planes)), dma((chunks, planes)),
            dma((chunks, group)), dma((chunks, group)),
        ],
        compiler_params=pltpu.CompilerParams(
            collective_id=0, has_side_effects=True, vmem_limit_bytes=50 * 2**20
        ),
        cost_estimate=pl.CostEstimate(
            flops=8 * rows * heads * dim * dim,
            bytes_accessed=8 * rows * heads * dim,
            transcendentals=0,
        ),
    )(queries, keys, values, decay_log.T)
    return normalize(mixed, scale, out_gain)


def solution(mesh):
    return jax.shard_map(
        functools.partial(shards, mesh.shape["ctx"], mesh.shape["head"]),
        mesh=mesh,
        in_specs=(
            P(("ctx", "head"), None, None),
            P(("ctx", "head"), None, None),
            P(("ctx", "head"), None, None),
            P(("ctx", "head"), None),
            P(),
        ),
        out_specs=P(("ctx", "head"), None, None),
        check_vma=False,
    )
```

```python
import functools

import jax
import jax.numpy as jnp
from jax import lax
from jax.experimental import pallas as pl
from jax.experimental.pallas import tpu as pltpu
from jax.sharding import PartitionSpec as P

F32, BF16 = jnp.float32, jnp.bfloat16
MESH = pl.DeviceIdType.MESH
TILE = 128


def plan(n_ctx, n_head, heads):
    inner = 1
    for option in (2, 4):
        if n_ctx % option == 0 and heads % (option * n_head) == 0:
            inner = option
    group = inner * n_head
    per_owner = heads // group
    chunks = 1
    for option in (2, 4):
        if per_owner % option == 0 and (heads // option) % 16 == 0:
            chunks = option
    return inner, group, per_owner, chunks


def silu(x):
    half = 0.5 * x
    return half + half * jnp.tanh(half)


def kernel(
    n_ctx, n_head, q_hbm, k_hbm, v_hbm, dec_ref, mix_ref, scale_ref,
    q_in, k_in, v_in, tmp_a, tmp_b, q_hm, k_hm, v_hm, cum_b, cum_t, end_b, intra,
    ends, ends_in, s_out, s_in, pre, tot_out, tot_in, t_out, t_in, come_x, i_out, i_in, squares,
    in_sem, e_send, e_recv, s_send, s_recv, d_send, d_recv, t_send, t_recv, i_send, i_recv,
):
    rows, heads, dim = q_hbm.shape
    inner, group, per_owner, chunks = plan(n_ctx, n_head, heads)
    width = heads // chunks
    hc = per_owner // chunks
    planes = n_ctx // inner
    ctx, head = lax.axis_index("ctx"), lax.axis_index("head")
    plane = ctx // inner
    place = ctx % inner
    me = place * n_head + head

    def device(peer):
        return (plane * inner + peer // n_head, peer % n_head)

    def peer_at(step):
        return lax.rem(me + step, group)

    def load(source, held, at, c):
        return pltpu.make_async_copy(
            source.at[:, pl.ds(c * width, width), :], held.at[c], in_sem.at[at, c]
        )

    load(k_hbm, k_in, 0, 0).start()
    load(v_hbm, v_in, 1, 0).start()

    barrier = pltpu.get_barrier_semaphore()

    def greet(step, carry):
        pl.semaphore_signal(barrier, inc=1, device_id=device(peer_at(step)), device_id_type=MESH)
        return carry

    lax.fori_loop(1, group, greet, 0)

    def greet_plane(step, carry):
        other = lax.rem(plane + step, planes)
        pl.semaphore_signal(
            barrier, inc=1, device_id=(other * inner + place, head), device_id_type=MESH
        )
        return carry

    lax.fori_loop(1, planes, greet_plane, 0)

    decays = dec_ref[...]
    t_at = lax.broadcasted_iota(jnp.int32, (rows, rows), 0)
    s_at = lax.broadcasted_iota(jnp.int32, (rows, rows), 1)
    lower = jnp.where(s_at <= t_at, 1.0, 0.0).astype(BF16)
    upper = jnp.where(t_at <= s_at, 1.0, 0.0).astype(BF16)
    over_rows = (((0,), (0,)), ((), ()))
    cum_t[...] = jnp.dot(decays, upper, preferred_element_type=F32)
    end_b[...] = jnp.dot(decays, jnp.ones((rows, dim), BF16), preferred_element_type=F32)
    squares[...] = jnp.zeros_like(squares)
    some = 8
    h_at = lax.broadcasted_iota(jnp.int32, (heads, some * dim), 0)
    l_at = lax.broadcasted_iota(jnp.int32, (heads, some * dim), 1) // dim

    def spread(g, carry):
        pick = jnp.where(h_at == l_at + g * some, 1.0, 0.0).astype(BF16)
        wide = lax.dot_general(
            decays, pick, over_rows, preferred_element_type=F32
        ).astype(BF16)
        summed = jnp.dot(lower, wide, preferred_element_type=F32)
        for i in range(some):
            cum_b[g * some + i] = summed[:, i * dim : (i + 1) * dim]
        return carry

    def remote(src, dst, send, recv, to):
        return pltpu.make_async_remote_copy(
            src_ref=src, dst_ref=dst, send_sem=send, recv_sem=recv,
            device_id=to, device_id_type=MESH,
        )

    def end_copy(peer, slot):
        return remote(ends.at[peer], ends_in.at[slot], e_send.at[peer], e_recv.at[slot], device(peer))

    def s_copy(c, peer, slot):
        return remote(
            s_out.at[c, peer], s_in.at[c, slot], s_send.at[c, peer], s_recv.at[c, slot], device(peer)
        )

    def i_copy(c, peer, slot):
        return remote(
            i_out.at[c, peer], i_in.at[c, slot], i_send.at[c, peer], i_recv.at[c, slot], device(peer)
        )

    def at_plane(other):
        return (other * inner + place, head)

    def d_copy(step, slot):
        other = lax.rem(plane + step, planes)
        return remote(tot_out, tot_in.at[slot], d_send.at[step], d_recv.at[slot], at_plane(other))

    def t_copy(c, step, slot):
        other = lax.rem(plane + step, planes)
        return remote(
            t_out.at[c], t_in.at[c, slot], t_send.at[c, step], t_recv.at[c, slot], at_plane(other)
        )

    def each_peer(body):
        def one(step, carry):
            body(peer_at(step))
            return carry

        lax.fori_loop(1, group, one, 0)

    def later_planes(body):
        for step in range(1, planes):
            @pl.when(plane + step < planes)
            def _():
                body(step)

    def earlier_planes(body):
        for p in range(planes - 1):
            @pl.when(p < plane)
            def _():
                body(p)

    step_rows = 16
    pitch = width + 1

    def activate(held, c, tmp):
        def some_rows(b, carry):
            x = silu(held[c, pl.ds(b * step_rows, step_rows)].astype(F32))
            base = pl.multiple_of(b * (step_rows * pitch), step_rows)
            for t in range(step_rows):
                tmp[pl.ds(base + t * pitch, width), :] = x[t]
            return carry

        lax.fori_loop(0, rows // step_rows, some_rows, 0)

    unroll = 8

    def each_head(c, body):
        def one(g, carry):
            for u in range(unroll):
                i = g * unroll + u
                body(i, c * width + i)
            return carry

        lax.fori_loop(0, width // unroll, one, 0)

    owners = max(1, unroll // hc)

    def each_owner(c, first, before, body, after):
        def one(g, carry):
            steps = [first + g * owners + u for u in range(owners)]
            for step in steps:
                before(step, peer_at(step))
            for step in steps:
                for u in range(hc):
                    i = peer_at(step) * hc + u
                    body(i, c * width + i, peer_at(step), u)
            for step in steps:
                after(step, peer_at(step))
            return carry

        lax.fori_loop(0, group // owners, one, 0)

    def nothing(step, peer):
        pass

    def states(c):
        lax.fori_loop(c * width // some, (c + 1) * width // some, spread, 0)
        load(k_hbm, k_in, 0, c).wait()
        load(v_hbm, v_in, 1, c).wait()
        if c + 1 < chunks:
            load(k_hbm, k_in, 0, c + 1).start()
            load(v_hbm, v_in, 1, c + 1).start()
        else:
            for at in range(chunks):
                load(q_hbm, q_in, 2, at).start()
        activate(k_in, c, tmp_a)
        activate(v_in, c, tmp_b)

        def one(i, h, peer, u):
            key = tmp_a[pl.ds(i, rows, stride=pitch), :].astype(BF16)
            value = tmp_b[pl.ds(i, rows, stride=pitch), :].astype(BF16)
            k_hm[h] = key
            v_hm[h] = value
            fade = jnp.exp(end_b[pl.ds(h, 1), :] - cum_b[h])
            scaled = (key.astype(F32) * fade).astype(BF16)
            state = lax.dot_general(scaled, value, over_rows, preferred_element_type=F32)
            s_out[c, peer, u * dim : (u + 1) * dim, :] = state.astype(BF16)

        if c == 0:
            pl.semaphore_wait(barrier, group + planes - 2)

        def send(step, peer):
            @pl.when(step < group)
            def _():
                s_copy(c, peer, me).start()

        each_owner(c, 1, nothing, one, send)
        if c == 0:
            for o in range(group):
                for d in range(chunks):
                    at = d * width + o * hc
                    ends[o, d * hc : (d + 1) * hc, :] = end_b[at : at + hc, :]
            each_peer(lambda peer: end_copy(peer, me).start())
            ends_in[me] = ends[me]
        s_in[c, me] = s_out[c, me]

    def inside(c):
        load(q_hbm, q_in, 2, c).wait()
        activate(q_in, c, tmp_a)

        def one(i, h):
            query = tmp_a[pl.ds(i, rows, stride=pitch), :].astype(BF16)
            q_hm[h] = query
            key, value, cum = k_hm[h], v_hm[h], cum_b[h]
            row = cum_t[pl.ds(h, 1), :]
            outs = []
            for s0 in range(0, rows, TILE):
                w = min(TILE, rows - s0)
                n = rows - s0
                scores = lax.dot_general(
                    query[s0:], key[s0 : s0 + w], (((1,), (1,)), ((), ())),
                    preferred_element_type=F32,
                )
                offset = cum[s0:, :w] - row[:, s0 : s0 + w]
                tt = lax.broadcasted_iota(jnp.int32, (w, w), 0)
                ss = lax.broadcasted_iota(jnp.int32, (w, w), 1)
                fades = jnp.exp(jnp.where(ss <= tt, offset[:w], -1e30))
                if n > w:
                    fades = jnp.concatenate([fades, jnp.exp(offset[w:])], axis=0)
                weights = scores * fades
                outs.append(
                    jnp.dot(
                        weights.astype(BF16), value[s0 : s0 + w], preferred_element_type=F32
                    )
                )
            intra[h] = outs[0]
            for at in range(1, len(outs)):
                intra[h, at * TILE :, :] += outs[at]

        each_head(c, one)

    def join(c):
        if c == 0:
            each_peer(lambda peer: end_copy(peer, peer).wait_recv())
            tot_out[...] = jnp.sum(ends_in[...], axis=0)
            later_planes(lambda step: d_copy(step, plane).start())
        each_peer(lambda peer: s_copy(c, peer, peer).wait_recv())
        for i in range(hc):
            part = pl.ds(i * dim, dim)
            at = c * hc + i
            total = s_in[c, 0, part, :].astype(F32)
            for j in range(1, group):
                pre[c, j, part, :] = total
                fade = jnp.exp(ends_in[j, at : at + 1, :])
                total = fade * total + s_in[c, j, part, :].astype(F32)
            t_out[c, part, :] = total.astype(BF16)
        later_planes(lambda step: t_copy(c, step, plane).start())

    def spread_out(c):
        if c == 0:
            earlier_planes(lambda p: d_copy(1, p).wait_recv())
        earlier_planes(lambda p: t_copy(c, 1, p).wait_recv())
        come_x[...] = jnp.zeros_like(come_x)

        def add(p):
            for i in range(hc):
                part = pl.ds(i * dim, dim)
                at = c * hc + i
                fade = jnp.exp(tot_in[p, at : at + 1, :])
                come_x[part, :] = fade * come_x[part, :] + t_in[c, p, part, :].astype(F32)

        earlier_planes(add)
        fades = [jnp.zeros((1, dim), F32)] * hc
        for j in range(group):
            for i in range(hc):
                part = pl.ds(i * dim, dim)
                at = c * hc + i
                come = come_x[part, :]
                if j > 0:
                    fades[i] = fades[i] + ends_in[j - 1, at : at + 1, :]
                    come = pre[c, j, part, :] + jnp.exp(fades[i]) * come
                i_out[c, j, part, :] = come.astype(BF16)

            @pl.when(j != me)
            def _():
                i_copy(c, j, me).start()

        i_in[c, me] = i_out[c, me]

    def finish(c):
        def arrive(step, peer):
            @pl.when(step > 0)
            def _():
                i_copy(c, peer, peer).wait_recv()

        def one(i, h, peer, u):
            come = i_in[c, peer, u * dim : (u + 1) * dim, :]
            inter = jnp.dot(q_hm[h], come, preferred_element_type=F32)
            mixed = (intra[h] + inter * jnp.exp(cum_b[h])).astype(BF16).astype(F32)
            squares[...] += mixed * mixed
            tmp_a[pl.ds(i, rows, stride=pitch), :] = mixed

        each_owner(c, 0, arrive, one, nothing)

        def some_rows(b, carry):
            base = pl.multiple_of(b * (step_rows * pitch), step_rows)
            for t in range(step_rows):
                mix_ref[b * step_rows + t, c * width : (c + 1) * width, :] = tmp_a[
                    pl.ds(base + t * pitch, width), :
                ].astype(BF16)
            return carry

        lax.fori_loop(0, rows // step_rows, some_rows, 0)

    ahead = 2
    for c in range(chunks):
        states(c)
        if c >= ahead:
            join(c - ahead)
    for c in range(max(chunks - ahead, 0), min(ahead, chunks)):
        join(c)
    for c in range(chunks):
        spread_out(c)
        inside(c)
        if c + ahead < chunks:
            join(c + ahead)
    for c in range(chunks):
        finish(c)
    meansq = jnp.sum(squares[...], axis=1, keepdims=True) * (1.0 / (heads * dim))
    scale_ref[...] = jnp.broadcast_to(lax.rsqrt(meansq + 1e-06), scale_ref.shape)

    each_peer(lambda peer: end_copy(peer, me).wait_send())
    later_planes(lambda step: d_copy(step, plane).wait_send())
    for c in range(chunks):
        each_peer(lambda peer: s_copy(c, peer, me).wait_send())
        each_peer(lambda peer: i_copy(c, peer, me).wait_send())
        later_planes(lambda step: t_copy(c, step, plane).wait_send())


def normalize(mixed, scale, out_gain):
    return (mixed.astype(F32) * scale[:, None, :] * out_gain[None]).astype(BF16)


def shards(n_ctx, n_head, queries, keys, values, decay_log, out_gain):
    rows, heads, dim = queries.shape
    inner, group, per_owner, chunks = plan(n_ctx, n_head, heads)
    width, hc = heads // chunks, per_owner // chunks
    held = pltpu.VMEM((chunks, rows, width, dim), BF16)
    major = pltpu.VMEM((heads, rows, dim), BF16)
    block = (hc * dim, dim)
    dma = pltpu.SemaphoreType.DMA
    planes = n_ctx // inner
    tile = (max(8, per_owner), dim)
    mixed, scale = pl.pallas_call(
        functools.partial(kernel, n_ctx, n_head),
        out_shape=(
            jax.ShapeDtypeStruct((rows, heads, dim), BF16),
            jax.ShapeDtypeStruct((rows, dim), F32),
        ),
        in_specs=[pl.BlockSpec(memory_space=pl.ANY)] * 3 + [pl.BlockSpec(memory_space=pltpu.VMEM)],
        out_specs=(pl.BlockSpec(memory_space=pltpu.VMEM),) * 2,
        scratch_shapes=[
            held, held, held,
            pltpu.VMEM((rows * (width + 1), dim), F32), pltpu.VMEM((rows * (width + 1), dim), F32),
            major, major, major,
            pltpu.VMEM((heads, rows, dim), F32),
            pltpu.VMEM((heads, rows), F32),
            pltpu.VMEM((heads, dim), F32),
            pltpu.VMEM((heads, rows, dim), F32),
            pltpu.VMEM((group,) + tile, F32), pltpu.VMEM((group,) + tile, F32),
            pltpu.VMEM((chunks, group) + block, BF16), pltpu.VMEM((chunks, group) + block, BF16),
            pltpu.VMEM((chunks, group) + block, F32),
            pltpu.VMEM(tile, F32), pltpu.VMEM((planes,) + tile, F32),
            pltpu.VMEM((chunks,) + block, BF16), pltpu.VMEM((chunks, planes) + block, BF16),
            pltpu.VMEM(block, F32),
            pltpu.VMEM((chunks, group) + block, BF16), pltpu.VMEM((chunks, group) + block, BF16),
            pltpu.VMEM((rows, dim), F32),
            dma((3, chunks)),
            dma((group,)), dma((group,)),
            dma((chunks, group)), dma((chunks, group)),
            dma((planes,)), dma((planes,)),
            dma((chunks, planes)), dma((chunks, planes)),
            dma((chunks, group)), dma((chunks, group)),
        ],
        compiler_params=pltpu.CompilerParams(
            collective_id=0, has_side_effects=True, vmem_limit_bytes=50 * 2**20
        ),
        cost_estimate=pl.CostEstimate(
            flops=8 * rows * heads * dim * dim,
            bytes_accessed=8 * rows * heads * dim,
            transcendentals=0,
        ),
    )(queries, keys, values, decay_log.T)
    return normalize(mixed, scale, out_gain)


def solution(mesh):
    return jax.shard_map(
        functools.partial(shards, mesh.shape["ctx"], mesh.shape["head"]),
        mesh=mesh,
        in_specs=(
            P(("ctx", "head"), None, None),
            P(("ctx", "head"), None, None),
            P(("ctx", "head"), None, None),
            P(("ctx", "head"), None),
            P(),
        ),
        out_specs=P(("ctx", "head"), None, None),
        check_vma=False,
    )
```
